512 devices in a mesh: fsdp: 64 (over z, x), tensor: 8 (over y, core).
Axes of the slice: x: 4, y: 4, z: 16, core: 2. Of those that a mesh axis runs over, the one named last changes fastest.
Arguments:
- momentum: float32 [8192, 26624], P('fsdp', 'tensor'), may hold values from -64 to 64
- gradient: bfloat16 [8192, 26624], P('fsdp', 'tensor'), may hold values from -6 to 6
- basis: float32 [256, 26624], P('fsdp', 'tensor'), may hold values from -0.0390625 to 0.0390625
Outputs:
- new_momentum: float32 [8192, 26624], P('fsdp', 'tensor')
- weight_delta: bfloat16 [8192, 26624], P('fsdp', 'tensor')
The draws below stay inside these ranges and needn't reach their ends.
All inputs are finite; a program needn't handle non-finite values.
Results may differ from the reference program's by a relative error of at most 0.003.
Values sent between devices are 32-bit elements; how exact they have to be, the bound alone decides.
A program may use at most 64 MiB of HBM per device.

```python
import jax
import jax.numpy as jnp
from jax import lax

ROWS = 8192
COLS = 26624
RANK = 256


def draw_momentum(key, part):
    key = jax.random.fold_in(key, 11)
    first = jax.random.fold_in(key, 0)
    row_pos = jnp.arange(ROWS, dtype=jnp.float32)[:, None] / ROWS
    col_pos = jnp.arange(COLS, dtype=jnp.float32)[None, :] / COLS
    base = jax.random.truncated_normal(first, -4.0, 4.0, (ROWS, COLS), jnp.float32)
    ramp = 10.0 ** col_pos * 3.0 ** row_pos / 4.0
    return base * ramp


def block_levels(key, shape, shards, low, top_value):
    gain = 1.0
    for axis_at, blocks in shards:
        heights = jax.random.uniform(jax.random.fold_in(jax.random.fold_in(key, 6), axis_at), (blocks,), jnp.float32, low / len(shards), top_value / len(shards))
        gain = gain * jnp.repeat(jnp.exp(heights), shape[axis_at] // blocks).reshape((-1,) + (1,) * (len(shape) - 1 - axis_at))
    return gain


def noise(key, shape, spread, reach, cuts=(), kind=jnp.bfloat16):
    result = spread * jax.random.normal(key, shape, jnp.float32)
    if cuts:
        result = result * block_levels(key, shape, cuts, -0.22, 0.18)
    return jnp.clip(result, -reach, reach).astype(kind)


def setup_inputs(seed: int = 0) -> dict:
    seeds = jax.random.split(jax.random.key(seed), 4)
    return {
        "momentum": draw_momentum(jax.random.fold_in(seeds[3], 71), 0),
        "gradient": noise(seeds[1], (ROWS, COLS), 1.0, 6.0, ((0, 64), (1, 8))),
        "basis": noise(seeds[2], (RANK, COLS), COLS ** -0.5, 0.0390625, ((0, 64), (1, 8)), jnp.float32),
    }


def reference(momentum, gradient, basis):
    high = lax.Precision.HIGHEST
    blend = momentum + gradient.astype(jnp.float32)
    proj = jnp.dot(blend.astype(jnp.float32), basis.T.astype(jnp.float32), precision=high, preferred_element_type=jnp.float32)
    gram = jnp.dot(proj.T.astype(jnp.float32), proj.astype(jnp.float32), precision=high, preferred_element_type=jnp.float32)
    lower = jnp.linalg.cholesky(gram)
    ortho = jax.scipy.linalg.solve_triangular(lower, proj.T, lower=True).T
    right = jnp.dot(ortho.T.astype(jnp.float32), blend.astype(jnp.float32), precision=high, preferred_element_type=jnp.float32)
    inverse = 1.0 / (jnp.sqrt(lax.optimization_barrier(jnp.sum(right * right, axis=1))) + 1e-06)
    feedback = jnp.dot(ortho.astype(jnp.float32), right.astype(jnp.float32), precision=high, preferred_element_type=jnp.float32)
    update = jnp.dot(ortho.astype(jnp.float32), (right * inverse[:, None]).astype(jnp.float32), precision=high, preferred_element_type=jnp.float32)
    new_momentum = blend - 0.05 * feedback
    factor = (ROWS * COLS / RANK) ** 0.5
    weight_delta = (-factor * update).astype(jnp.bfloat16)
    return (new_momentum, weight_delta)
```

```python
import functools

import jax
import jax.numpy as jnp
from jax import lax
from jax.experimental import pallas as pl
from jax.experimental.pallas import tpu as pltpu
from jax.sharding import PartitionSpec as P

ROWS = 8192
COLS = 26624
RANK = 256
NX = 4
GROUPS = RANK // 4
PANEL = 32
F32 = jnp.float32
BF16 = jnp.bfloat16
HIGHEST = lax.Precision.HIGHEST
NT = (((1,), (1,)), ((), ()))
TN = (((0,), (0,)), ((), ()))
NN = (((1,), (0,)), ((), ()))


def split(value):
    high = value.astype(BF16)
    return high, (value - high.astype(F32)).astype(BF16)


def dot(a, b, dims):
    return lax.dot_general(a, b, dims, preferred_element_type=F32)


def dot3(a, b, dims):
    (ah, al), (bh, bl) = a, b
    return dot(ah, bh, dims) + (dot(ah, bl, dims) + dot(al, bh, dims))


def dot_full(a, b, dims):
    return lax.dot_general(a, b, dims, precision=HIGHEST, preferred_element_type=F32)


def kernel(
    nz, nt, factor,
    mom_hbm, grad_hbm, basis_hbm, newm_hbm, delta_hbm,
    mom, grad, bhi, blo, vbuf, part, proj, rsbuf,
    wbuf, ropp, rleft, rright, rz, wfin,
    gram, gslice, grs, gsum, gx, gall, elim,
    rhi, rlo, nbuf, dout,
    load_sem, store_sem, v_send, v_z, v_l, v_r, v_o,
    w_send, w_z, w_l, w_r, w_o, r_send, r_z, r_l, r_r, r_o,
    s_send, s_recv,
):
    rows, cols = mom.shape
    nblk = cols // 128
    nh = nblk // 2
    half = nz // 2
    m = GROUPS // (nz * NX)
    f = lax.axis_index("fsdp")
    t = lax.axis_index("tensor")
    z, x = lax.div(f, NX), lax.rem(f, NX)
    left, right, opp = lax.rem(x + NX - 1, NX), lax.rem(x + 1, NX), lax.rem(x + 2, NX)

    def zmod(value):
        return lax.rem(value + nz, nz)

    def tmod(value):
        return lax.rem(value + nt, nt)

    def dev(zz, xx):
        return (zz * NX + xx, t)

    to_up, to_down = dev(zmod(z + 1), x), dev(zmod(z - 1), x)
    to_left, to_right, to_opp = dev(z, left), dev(z, right), dev(z, opp)

    def remote(src, dst, send, recv, device):
        return pltpu.make_async_remote_copy(
            src_ref=src, dst_ref=dst, send_sem=send, recv_sem=recv,
            device_id=device, device_id_type=pl.DeviceIdType.MESH,
        )

    def wait(ref, sem):
        pltpu.make_async_copy(ref, ref, sem).wait()

    load_basis = pltpu.make_async_copy(basis_hbm, vbuf.at[pl.ds(f * m, m)], load_sem.at[0])
    load_mom = pltpu.make_async_copy(mom_hbm, mom, load_sem.at[1])
    load_grad = pltpu.make_async_copy(grad_hbm, grad, load_sem.at[2])
    load_basis.start()
    load_mom.start()
    load_grad.start()

    barrier = pltpu.get_barrier_semaphore()

    def greet(device):
        pl.semaphore_signal(barrier, inc=1, device_id=device, device_id_type=pl.DeviceIdType.MESH)

    def greet_z(r, carry):
        greet(dev(zmod(z + r), x))
        return carry

    def greet_t(r, carry):
        greet((f, tmod(t + r)))
        return carry

    lax.fori_loop(1, nz, greet_z, 0)
    lax.fori_loop(1, nt, greet_t, 0)
    for device in (to_left, to_right, to_opp):
        greet(device)
    pl.semaphore_wait(barrier, (nz - 1) + (nt - 1) + 3)

    def gather(buf, send, sz, sl, sr, so, early, hook):
        def at(zz, xx):
            return buf.at[pl.ds((zz * NX + xx) * m, m)]

        def push(zz, xx, sem, device):
            remote(at(zz, xx), at(zz, xx), send, sem.at[zz], device).start()

        def spread(zz):
            push(zz, x, sl, to_right)
            push(zz, x, sr, to_left)

        def pass_right(zz):
            wait(at(zz, left), sl.at[zz])
            push(zz, left, so, to_right)

        def pass_left(zz):
            wait(at(zz, right), sr.at[zz])
            push(zz, right, so, to_left)

        push(z, x, sz, to_up)
        if half > 1:
            push(z, x, sz, to_down)
        spread(z)
        early()

        def step(j, carry):
            below, above = zmod(z - j), zmod(z + j)
            wait(at(below, x), sz.at[below])

            @pl.when(j < half)
            def _():
                push(below, x, sz, to_up)

            spread(below)

            @pl.when(j < half)
            def _():
                wait(at(above, x), sz.at[above])

                @pl.when(j < half - 1)
                def _():
                    push(above, x, sz, to_down)

                spread(above)

            pass_right(zmod(z - j + 1))

            @pl.when(j > 1)
            def _():
                pass_left(zmod(z + j - 1))

            hook(j)
            return carry

        lax.fori_loop(1, half + 1, step, 0)
        pass_right(zmod(z - half))

        def finish(j, carry):
            below, above = zmod(z - j), zmod(z + j)
            wait(at(below, right), sr.at[below])
            wait(at(below, opp), so.at[below])

            @pl.when((j > 0) & (j < half))
            def _():
                wait(at(above, left), sl.at[above])
                wait(at(above, opp), so.at[above])

            return carry

        lax.fori_loop(0, half + 1, finish, 0)
        wait(buf.at[pl.ds(0, (nz * NX - 1) * m)], send)

    load_basis.wait()

    def make_blend():
        load_mom.wait()
        load_grad.wait()

        def body(c, carry):
            cut = pl.ds(pl.multiple_of(c * 256, 256), 256)
            blend = mom[:, cut] + grad[:, cut].astype(F32)
            mom[:, cut] = blend
            bhi[:, cut], blo[:, cut] = split(blend)
            return carry

        lax.fori_loop(0, nblk // 2, body, 0)

    gather(vbuf, v_send.at[0], v_z, v_l, v_r, v_o, make_blend, lambda j: None)

    def project(c, acc):
        cut = pl.ds(pl.multiple_of(c * 256, 256), 256)
        pair = [vbuf[:, 2 * c + k].reshape(RANK, 128) for k in range(2)]
        return acc + dot3((bhi[:, cut], blo[:, cut]), split(jnp.concatenate(pair, axis=1)), NT)

    part[...] = lax.fori_loop(0, nblk // 2, project, jnp.zeros((rows, RANK), F32))

    share = rows // nt
    if nt > 1:
        own = pl.ds(t * share, share)

        def send_part(r, carry):
            peer = tmod(t + r)
            remote(
                part.at[pl.ds(peer * share, share)], rsbuf.at[r - 1],
                s_send.at[0], s_recv.at[0], (f, peer),
            ).start()
            return carry

        lax.fori_loop(1, nt, send_part, 0)
        wait(rsbuf, s_recv.at[0])
        total = part[own]
        for r in range(nt - 1):
            total = total + rsbuf[r]
        proj[own] = total

        def send_sum(r, carry):
            remote(
                proj.at[own], proj.at[own], s_send.at[1], s_recv.at[1], (f, tmod(t + r))
            ).start()
            return carry

        lax.fori_loop(1, nt, send_sum, 0)
        wait(proj.at[pl.ds(0, (nt - 1) * share)], s_recv.at[1])
        wait(rsbuf, s_send.at[0])
        wait(proj.at[pl.ds(0, (nt - 1) * share)], s_send.at[1])
    else:
        proj[...] = part[...]

    full = proj[...]
    gram[...] = dot_full(full, full, TN)
    gshare = RANK // nt
    ng = 2 * gshare // 4
    mg = ng // nz
    mine = gram[pl.ds(t * gshare, gshare), :]
    for r in range(gshare // 4):
        for c in range(2):
            gslice[2 * r + c] = mine[4 * r : 4 * r + 4, 128 * c : 128 * c + 128]

    def gram_send():
        def body(r, carry):
            peer = zmod(z + r)
            remote(
                gslice.at[pl.ds(peer * mg, mg)], grs.at[r - 1],
                s_send.at[2], s_recv.at[2], dev(peer, x),
            ).start()
            return carry

        lax.fori_loop(1, nz, body, 0)

    def gram_over_z():
        wait(grs, s_recv.at[2])
        gsum[...] = gslice[pl.ds(z * mg, mg)] + jnp.sum(grs[...], axis=0)
        gx[x] = gsum[...]
        for k, device in enumerate((to_left, to_right, to_opp)):
            remote(gsum, gx.at[x], s_send.at[3], s_recv.at[3], device).start()

    def gram_over_x():
        wait(gx.at[pl.ds(0, NX - 1)], s_recv.at[3])
        here = pl.ds(t * ng + z * mg, mg)
        gall[here] = jnp.sum(gx[...], axis=0)

        def body(r, carry):
            remote(
                gall.at[here], gall.at[here], s_send.at[4], s_recv.at[4], dev(zmod(z + r), x)
            ).start()
            return carry

        lax.fori_loop(1, nz, body, 0)

    def gram_over_t():
        wait(gall.at[pl.ds(0, (nz - 1) * mg)], s_recv.at[4])
        if nt > 1:
            here = pl.ds(t * ng, ng)

            def body(r, carry):
                remote(
                    gall.at[here], gall.at[here], s_send.at[5], s_recv.at[5], (f, tmod(t + r))
                ).start()
                return carry

            lax.fori_loop(1, nt, body, 0)

    def gram_done():
        if nt > 1:
            wait(gall.at[pl.ds(0, (nt - 1) * ng)], s_recv.at[5])
            wait(gall.at[pl.ds(0, (nt - 1) * ng)], s_send.at[5])
        wait(grs, s_send.at[2])
        wait(gx.at[pl.ds(0, NX - 1)], s_send.at[3])
        wait(gall.at[pl.ds(0, (nz - 1) * mg)], s_send.at[4])
        for r in range(RANK // 8):
            for c in range(2):
                pair = [gall[4 * r + c], gall[4 * r + 2 + c]]
                elim[8 * r : 8 * r + 8, 128 * c : 128 * c + 128] = jnp.concatenate(pair, axis=0)
        down = lax.broadcasted_iota(jnp.int32, (RANK, RANK), 0)
        across = lax.broadcasted_iota(jnp.int32, (RANK, RANK), 1)
        elim[:, RANK:] = jnp.where(down == across, 1.0, 0.0).astype(F32)

    gram_send()

    turned = split(full.T)
    for h in range(2):
        start = 0
        while start < nh:
            width = min(4, nh - start) if nh - start != 5 else 5
            cut = slice((h * nh + start) * 128, (h * nh + start + width) * 128)
            out = dot3(turned, (bhi[:, cut], blo[:, cut]), NN)
            for k in range(width):
                for r in range(RANK // 8):
                    wbuf[2 * r + h, start + k] = out[8 * r : 8 * r + 8, 128 * k : 128 * k + 128]
            start += width

    def piece(buf, index):
        return buf.at[pl.ds(index * m, m)]

    def wat(q, xx):
        return piece(wbuf, q * NX + xx)

    def add_into(ref, other):
        ref[...] = ref[...] + other[...]

    def stage_a(q, s):
        remote(wat(q, opp), piece(ropp, q), r_send.at[0], r_o.at[q], (to_right, to_left)[s]).start()

    def stage_b(q, s):
        wait(piece(ropp, q), r_o.at[q])
        add_into(wat(q, (right, left)[s]), piece(ropp, q))
        remote(wat(q, right), piece(rleft, q), r_send.at[0], r_l.at[q], to_right).start()
        remote(wat(q, left), piece(rright, q), r_send.at[0], r_r.at[q], to_left).start()

    def stage_c(q):
        wait(piece(rleft, q), r_l.at[q])
        wait(piece(rright, q), r_r.at[q])
        here = wat(q, x)
        here[...] = here[...] + (piece(rleft, q)[...] + piece(rright, q)[...])

    def stage_z(q, slot, device):
        remote(wat(q, x), piece(rz, slot), r_send.at[0], r_z.at[slot], device).start()

    def take_z(q, slot):
        wait(piece(rz, slot), r_z.at[slot])
        add_into(wat(q, x), piece(rz, slot))

    def reduce_step(i, carry):
        @pl.when(i <= half)
        def _():
            stage_a(zmod(z - half + i), 0)

        @pl.when((i >= 1) & (i < half))
        def _():
            stage_a(zmod(z + half - i), 1)

        b = i - 1

        @pl.when((b >= 0) & (b <= half))
        def _():
            stage_b(zmod(z - half + b), 0)

        @pl.when((b >= 1) & (b < half))
        def _():
            stage_b(zmod(z + half - b), 1)

        c = i - 2

        @pl.when(c >= 0)
        def _():
            q = zmod(z - half + c)
            stage_c(q)

            @pl.when(c > 0)
            def _():
                take_z(q, q)

            @pl.when(c < half)
            def _():
                stage_z(q, q, to_down)

        @pl.when((c >= 1) & (c < half))
        def _():
            q = zmod(z + half - c)
            stage_c(q)

            @pl.when(c > 1)
            def _():
                take_z(q, q)

            stage_z(q, lax.select(c == half - 1, nz, q), to_up)

        if half > 1:
            @pl.when(c == half)
            def _():
                take_z(z, nz)

        @pl.when(i == max(1, half // 4))
        def _():
            gram_over_z()

        @pl.when(i == max(2, half // 2))
        def _():
            gram_over_x()

        @pl.when(i == max(3, 3 * half // 4))
        def _():
            gram_over_t()

        return carry

    lax.fori_loop(0, half + 3, reduce_step, 0)
    piece(wfin, f)[...] = wat(z, x)[...]
    gram_done()

    lane = lax.broadcasted_iota(jnp.int32, (PANEL, 128), 1)
    down = lax.broadcasted_iota(jnp.int32, (PANEL, 128), 0)
    wide = lax.broadcasted_iota(jnp.int32, (PANEL, RANK), 1)
    npanel = RANK // PANEL

    def panel(b):
        here = pl.ds(pl.multiple_of(b * PANEL, PANEL), PANEL)
        block = elim[here, :]
        turned = pltpu.roll(block[:, :RANK], lax.rem(RANK - b * PANEL, RANK), 1)[:, :128]
        state = jnp.where(lane < PANEL, turned, jnp.where(lane == down + PANEL, 1.0, 0.0))
        for j in range(PANEL - 1):
            row = state[j : j + 1, :]
            scale = state[:, j : j + 1] / state[j : j + 1, j : j + 1]
            state = state - jnp.where(down > j, scale, 0.0) * row
        diag = jnp.sum(jnp.where(lane == down, state, 0.0), axis=1, keepdims=True)
        lower = state[:, PANEL : 2 * PANEL] / jnp.sqrt(diag)
        done = dot_full(lower, block, NN)
        rest = jnp.where(wide >= (b + 1) * PANEL, done[:, :RANK], 0.0)
        elim[...] = elim[...] - dot_full(rest, done, TN)
        elim[here, :] = done

    def panels(j):
        for k in range(npanel // half):
            panel((j - 1) * (npanel // half) + k)

    gather(wfin, w_send.at[0], w_z, w_l, w_r, w_o, lambda: None, panels)
    wait(wbuf.at[pl.ds(0, (nz * NX - 1) * m)], r_send.at[0])

    inv_lower = elim[:, RANK:]
    ortho = dot_full(proj[...], inv_lower, NT)
    low = split(inv_lower)
    squared = jnp.zeros((RANK, 128), F32)
    cuts = []
    for h in range(2):
        start = 0
        while start < nh:
            width = min(4, nh - start) if nh - start != 5 else 5
            cuts.append((h, start, width))
            start += width
    for h, start, width in cuts:
        cut = slice((h * nh + start) * 128, (h * nh + start + width) * 128)
        columns = [
            jnp.concatenate([wfin[2 * r + h, start + k] for r in range(RANK // 8)], axis=0)
            for k in range(width)
        ]
        out = dot3(low, split(jnp.concatenate(columns, axis=1)), NN)
        for k in range(width):
            one = out[:, 128 * k : 128 * k + 128]
            squared = squared + one * one
        rhi[:, cut], rlo[:, cut] = split(out)
    nbuf[t] = dot_full(jnp.ones((8, 128), F32), squared, NT)

    if nt > 1:
        def send_norm(r, carry):
            remote(
                nbuf.at[t], nbuf.at[t], s_send.at[6], s_recv.at[6], (f, tmod(t + r))
            ).start()
            return carry

        lax.fori_loop(1, nt, send_norm, 0)

    ortho_high = ortho.astype(BF16)
    stores = []
    for n, (h, start, width) in enumerate(cuts):
        cut = slice((h * nh + start) * 128, (h * nh + start + width) * 128)
        mom[:, cut] = mom[:, cut] - 0.05 * dot(ortho_high, rhi[:, cut], NN)
        stores.append(pltpu.make_async_copy(mom.at[:, cut], newm_hbm.at[:, cut], store_sem.at[n]))
        stores[-1].start()

    if nt > 1:
        wait(nbuf.at[pl.ds(0, nt - 1)], s_recv.at[6])
        wait(nbuf.at[pl.ds(0, nt - 1)], s_send.at[6])
    norm = nbuf[0]
    for r in range(1, nt):
        norm = norm + nbuf[r]
    inverse = 1.0 / (jnp.sqrt(norm) + 1e-06)
    scaled = split(ortho * (inverse[0:1, :] * -factor))
    for n, (h, start, width) in enumerate(cuts):
        cut = slice((h * nh + start) * 128, (h * nh + start + width) * 128)
        dout[:, cut] = dot3(scaled, (rhi[:, cut], rlo[:, cut]), NN).astype(BF16)
        stores.append(
            pltpu.make_async_copy(dout.at[:, cut], delta_hbm.at[:, cut], store_sem.at[len(cuts) + n])
        )
        stores[-1].start()
    for store in stores:
        store.wait()


def per_device(nz, nt, factor, momentum, gradient, basis):
    rows, cols = momentum.shape
    nblk = cols // 128
    nh = nblk // 2
    m = GROUPS // (nz * NX)
    gshare = RANK // nt
    ng = 2 * gshare // 4
    mg = ng // nz
    tiles = basis.reshape(m, 4, nblk, 128).transpose(0, 2, 1, 3)
    vmem = pltpu.VMEM
    dma = pltpu.SemaphoreType.DMA
    any_spec = pl.BlockSpec(memory_space=pl.ANY)
    one = max(nt - 1, 1)
    return pl.pallas_call(
        functools.partial(kernel, nz, nt, factor),
        out_shape=(
            jax.ShapeDtypeStruct((rows, cols), F32),
            jax.ShapeDtypeStruct((rows, cols), BF16),
        ),
        in_specs=[any_spec] * 3,
        out_specs=(any_spec, any_spec),
        scratch_shapes=[
            vmem((rows, cols), F32),
            vmem((rows, cols), BF16),
            vmem((rows, cols), BF16),
            vmem((rows, cols), BF16),
            vmem((GROUPS, nblk, 4, 128), F32),
            vmem((rows, RANK), F32),
            vmem((rows, RANK), F32),
            vmem((one, rows // nt, RANK), F32),
            vmem((GROUPS, nh, 8, 128), F32),
            vmem((nz * m, nh, 8, 128), F32),
            vmem((nz * m, nh, 8, 128), F32),
            vmem((nz * m, nh, 8, 128), F32),
            vmem(((nz + 1) * m, nh, 8, 128), F32),
            vmem((GROUPS, nh, 8, 128), F32),
            vmem((RANK, RANK), F32),
            vmem((ng, 4, 128), F32),
            vmem((nz - 1, mg, 4, 128), F32),
            vmem((mg, 4, 128), F32),
            vmem((NX, mg, 4, 128), F32),
            vmem((2 * GROUPS, 4, 128), F32),
            vmem((RANK, 2 * RANK), F32),
            vmem((RANK, cols), BF16),
            vmem((RANK, cols), BF16),
            vmem((nt, 8, RANK), F32),
            vmem((rows, cols), BF16),
            dma((3,)),
            dma((16,)),
            dma((1,)), dma((nz,)), dma((nz,)), dma((nz,)), dma((nz,)),
            dma((1,)), dma((nz,)), dma((nz,)), dma((nz,)), dma((nz,)),
            dma((1,)), dma((nz + 1,)), dma((nz,)), dma((nz,)), dma((nz,)),
            dma((7,)),
            dma((7,)),
        ],
        compiler_params=pltpu.CompilerParams(
            collective_id=0, has_side_effects=True, vmem_limit_bytes=56 * 2**20
        ),
        name="dion_step",
    )(momentum, gradient, tiles)


def solution(mesh):
    nz, nt = mesh.shape["fsdp"] // NX, mesh.shape["tensor"]
    factor = (ROWS * COLS / RANK) ** 0.5
    spec = P("fsdp", "tensor")
    return jax.shard_map(
        functools.partial(per_device, nz, nt, factor),
        mesh=mesh, in_specs=(spec,) * 3, out_specs=(spec,) * 2, check_vma=False,
    )
```

```python
import functools

import jax
import jax.numpy as jnp
from jax import lax
from jax.experimental import pallas as pl
from jax.experimental.pallas import tpu as pltpu
from jax.sharding import PartitionSpec as P

ROWS = 8192
COLS = 26624
RANK = 256
NX = 4
GROUPS = RANK // 4
PANEL = 32
MINI = 16
F32 = jnp.float32
BF16 = jnp.bfloat16
HIGHEST = lax.Precision.HIGHEST
NT = (((1,), (1,)), ((), ()))
TN = (((0,), (0,)), ((), ()))
NN = (((1,), (0,)), ((), ()))


def split3(value):
    high = value.astype(BF16)
    rest = value - high.astype(F32)
    mid = rest.astype(BF16)
    return high, mid, (rest - mid.astype(F32)).astype(BF16)


def split(value):
    high = value.astype(BF16)
    return high, (value - high.astype(F32)).astype(BF16)


def dot(a, b, dims):
    return lax.dot_general(a, b, dims, preferred_element_type=F32)


def dot3(a, b, dims):
    (ah, al), (bh, bl) = a, b
    return dot(ah, bh, dims) + (dot(ah, bl, dims) + dot(al, bh, dims))


def dot_full(a, b, dims):
    return lax.dot_general(a, b, dims, precision=HIGHEST, preferred_element_type=F32)


def kernel(
    nz, nt, factor,
    mom_hbm, grad_hbm, basis_hbm, newm_hbm, delta_hbm,
    mom, grad, bhi, blo, vbuf, part, proj, rsbuf,
    wbuf, ropp, rleft, rright, rodd, reven, aodd, aeven, across, wfin,
    gram, gslice, grs, gsum, gx, gall, elim,
    rhi, rlo, nbuf, dout,
    load_sem, store_sem, v_send, v_z, v_l, v_r, v_o, v_a,
    w_send, w_z, w_l, w_r, w_o, w_a, r_send, r_odd, r_even, a_odd, a_even, r_l, r_r, r_o,
    s_send, s_recv,
):
    rows, cols = mom.shape
    nblk = cols // 128
    nh = nblk // 2
    half = nz // 2
    na = across.shape[1]
    nb = nh - na
    m = GROUPS // (nz * NX)
    f = lax.axis_index("fsdp")
    t = lax.axis_index("tensor")
    z, x = lax.div(f, NX), lax.rem(f, NX)
    left, right, opp = lax.rem(x + NX - 1, NX), lax.rem(x + 1, NX), lax.rem(x + 2, NX)

    def zmod(value):
        return lax.rem(value + nz, nz)

    def tmod(value):
        return lax.rem(value + nt, nt)

    def dev(zz, xx):
        return (zz * NX + xx, t)

    to_up, to_down = dev(zmod(z + 1), x), dev(zmod(z - 1), x)
    to_up2, to_down2 = dev(zmod(z + 2), x), dev(zmod(z - 2 + nz), x)
    to_left, to_right, to_opp = dev(z, left), dev(z, right), dev(z, opp)

    def remote(src, dst, send, recv, device):
        return pltpu.make_async_remote_copy(
            src_ref=src, dst_ref=dst, send_sem=send, recv_sem=recv,
            device_id=device, device_id_type=pl.DeviceIdType.MESH,
        )

    def wait(ref, sem):
        pltpu.make_async_copy(ref, ref, sem).wait()

    load_basis = pltpu.make_async_copy(basis_hbm, vbuf.at[pl.ds(f * m, m)], load_sem.at[0])
    load_mom = pltpu.make_async_copy(mom_hbm, mom, load_sem.at[1])
    load_grad = pltpu.make_async_copy(grad_hbm, grad, load_sem.at[2])
    load_basis.start()
    load_mom.start()
    load_grad.start()

    barrier = pltpu.get_barrier_semaphore()

    def greet(device):
        pl.semaphore_signal(barrier, inc=1, device_id=device, device_id_type=pl.DeviceIdType.MESH)

    def greet_z(r, carry):
        greet(dev(zmod(z + r), x))
        return carry

    def greet_t(r, carry):
        greet((f, tmod(t + r)))
        return carry

    lax.fori_loop(1, nz, greet_z, 0)
    lax.fori_loop(1, nt, greet_t, 0)
    for device in (to_left, to_right, to_opp):
        greet(device)
    pl.semaphore_wait(barrier, (nz - 1) + (nt - 1) + 3)

    def gather(buf, cut, send, sz, sl, sr, so, sa, early, hook):
        whole = buf.shape[1]

        def at(zz, xx):
            return buf.at[pl.ds((zz * NX + xx) * m, m), pl.ds(0, cut)]

        def late(zz, xx):
            return buf.at[pl.ds((zz * NX + xx) * m, m), pl.ds(cut, whole - cut)]

        def bundle(zz):
            return buf.at[pl.ds(zz * NX * m, NX * m), pl.ds(cut, whole - cut)]

        def onward(j, ref, sem):
            @pl.when(j + 1 <= half)
            def _():
                remote(ref, ref, send, sem, to_up).start()

            @pl.when(j + 2 <= half)
            def _():
                remote(ref, ref, send, sem, to_up2).start()

        def back(j, ref, sem):
            @pl.when(j + 1 < half)
            def _():
                remote(ref, ref, send, sem, to_down).start()

            @pl.when(j + 2 < half)
            def _():
                remote(ref, ref, send, sem, to_down2).start()

        def push(zz, xx, sem, device):
            remote(at(zz, xx), at(zz, xx), send, sem.at[zz], device).start()

        def spread(zz):
            push(zz, x, sl, to_right)
            push(zz, x, sr, to_left)

        def pass_right(zz):
            wait(at(zz, left), sl.at[zz])
            push(zz, left, so, to_right)

        def pass_left(zz):
            wait(at(zz, right), sr.at[zz])
            push(zz, right, so, to_left)

        for device in (to_right, to_left, to_opp):
            remote(late(z, x), late(z, x), send, sa.at[nz], device).start()
        onward(0, at(z, x), sz.at[z])
        back(0, at(z, x), sz.at[z])
        spread(z)
        early()
        wait(buf.at[pl.ds(0, (NX - 1) * m), pl.ds(cut, whole - cut)], sa.at[nz])
        onward(0, bundle(z), sa.at[z])
        back(0, bundle(z), sa.at[z])

        def step(j, carry):
            below, above = zmod(z - j), zmod(z + j)
            even = lax.rem(j, 2) == 0
            wait(at(below, x), sz.at[below])

            @pl.when(even)
            def _():
                onward(j, at(below, x), sz.at[below])

            spread(below)

            @pl.when(j < half)
            def _():
                wait(at(above, x), sz.at[above])

                @pl.when(even)
                def _():
                    back(j, at(above, x), sz.at[above])

                spread(above)

            wait(bundle(below), sa.at[below])

            @pl.when(even)
            def _():
                onward(j, bundle(below), sa.at[below])

            @pl.when(j < half)
            def _():
                wait(bundle(above), sa.at[above])

                @pl.when(even)
                def _():
                    back(j, bundle(above), sa.at[above])

            pass_right(zmod(z - j + 1))

            @pl.when(j > 1)
            def _():
                pass_left(zmod(z + j - 1))

            hook(j)
            return carry

        lax.fori_loop(1, half + 1, step, 0)
        pass_right(zmod(z - half))

        def finish(j, carry):
            below, above = zmod(z - j), zmod(z + j)
            wait(at(below, right), sr.at[below])
            wait(at(below, opp), so.at[below])

            @pl.when((j > 0) & (j < half))
            def _():
                wait(at(above, left), sl.at[above])
                wait(at(above, opp), so.at[above])

            return carry

        lax.fori_loop(0, half + 1, finish, 0)
        wait(buf.at[pl.ds(0, (nz * NX - 1) * m)], send)

    load_basis.wait()

    def make_blend():
        load_mom.wait()
        load_grad.wait()

        def body(c, carry):
            cut = pl.ds(pl.multiple_of(c * 256, 256), 256)
            blend = mom[:, cut] + grad[:, cut].astype(F32)
            mom[:, cut] = blend
            bhi[:, cut], blo[:, cut] = split(blend)
            return carry

        lax.fori_loop(0, nblk // 2, body, 0)

    gather(vbuf, 2 * nb, v_send.at[0], v_z, v_l, v_r, v_o, v_a, make_blend, lambda j: None)

    def project(c, acc):
        cut = pl.ds(pl.multiple_of(c * 256, 256), 256)
        pair = [vbuf[:, 2 * c + k].reshape(RANK, 128) for k in range(2)]
        return acc + dot3((bhi[:, cut], blo[:, cut]), split(jnp.concatenate(pair, axis=1)), NT)

    part[...] = lax.fori_loop(0, nblk // 2, project, jnp.zeros((rows, RANK), F32))

    share = rows // nt
    if nt > 1:
        own = pl.ds(t * share, share)

        def send_part(r, carry):
            peer = tmod(t + r)
            remote(
                part.at[pl.ds(peer * share, share)], rsbuf.at[r - 1],
                s_send.at[0], s_recv.at[0], (f, peer),
            ).start()
            return carry

        lax.fori_loop(1, nt, send_part, 0)
        wait(rsbuf, s_recv.at[0])
        total = part[own]
        for r in range(nt - 1):
            total = total + rsbuf[r]
        proj[own] = total

        def send_sum(r, carry):
            remote(
                proj.at[own], proj.at[own], s_send.at[1], s_recv.at[1], (f, tmod(t + r))
            ).start()
            return carry

        lax.fori_loop(1, nt, send_sum, 0)
        wait(proj.at[pl.ds(0, (nt - 1) * share)], s_recv.at[1])
        wait(rsbuf, s_send.at[0])
        wait(proj.at[pl.ds(0, (nt - 1) * share)], s_send.at[1])
    else:
        proj[...] = part[...]

    full = proj[...]
    gram[...] = dot_full(full, full, TN)
    gshare = RANK // nt
    ng = 2 * gshare // 4
    mg = ng // nz
    mine = gram[pl.ds(t * gshare, gshare), :]
    for r in range(gshare // 4):
        for c in range(2):
            gslice[2 * r + c] = mine[4 * r : 4 * r + 4, 128 * c : 128 * c + 128]

    def gram_send():
        def body(r, carry):
            peer = zmod(z + r)
            remote(
                gslice.at[pl.ds(peer * mg, mg)], grs.at[r - 1],
                s_send.at[2], s_recv.at[2], dev(peer, x),
            ).start()
            return carry

        lax.fori_loop(1, nz, body, 0)

    def gram_over_z():
        wait(grs, s_recv.at[2])
        gsum[...] = gslice[pl.ds(z * mg, mg)] + jnp.sum(grs[...], axis=0)
        gx[x] = gsum[...]
        for k, device in enumerate((to_left, to_right, to_opp)):
            remote(gsum, gx.at[x], s_send.at[3], s_recv.at[3], device).start()

    def gram_over_x():
        wait(gx.at[pl.ds(0, NX - 1)], s_recv.at[3])
        here = pl.ds(t * ng + z * mg, mg)
        gall[here] = jnp.sum(gx[...], axis=0)

        def body(r, carry):
            remote(
                gall.at[here], gall.at[here], s_send.at[4], s_recv.at[4], dev(zmod(z + r), x)
            ).start()
            return carry

        lax.fori_loop(1, nz, body, 0)

    def gram_over_t():
        wait(gall.at[pl.ds(0, (nz - 1) * mg)], s_recv.at[4])
        if nt > 1:
            here = pl.ds(t * ng, ng)

            def body(r, carry):
                remote(
                    gall.at[here], gall.at[here], s_send.at[5], s_recv.at[5], (f, tmod(t + r))
                ).start()
                return carry

            lax.fori_loop(1, nt, body, 0)

    def gram_done():
        if nt > 1:
            wait(gall.at[pl.ds(0, (nt - 1) * ng)], s_recv.at[5])
            wait(gall.at[pl.ds(0, (nt - 1) * ng)], s_send.at[5])
        wait(grs, s_send.at[2])
        wait(gx.at[pl.ds(0, NX - 1)], s_send.at[3])
        wait(gall.at[pl.ds(0, (nz - 1) * mg)], s_send.at[4])
        for r in range(RANK // 8):
            for c in range(2):
                pair = [gall[4 * r + c], gall[4 * r + 2 + c]]
                elim[8 * r : 8 * r + 8, 128 * c : 128 * c + 128] = jnp.concatenate(pair, axis=0)
        down = lax.broadcasted_iota(jnp.int32, (RANK, RANK), 0)
        across = lax.broadcasted_iota(jnp.int32, (RANK, RANK), 1)
        elim[:, RANK:] = jnp.where(down == across, 1.0, 0.0).astype(F32)

    gram_send()

    turned = split(full.T)
    for h in range(2):
        start = 0
        while start < nh:
            width = min(4, nh - start) if nh - start != 5 else 5
            cut = slice((h * nh + start) * 128, (h * nh + start + width) * 128)
            out = dot3(turned, (bhi[:, cut], blo[:, cut]), NN)
            for k in range(width):
                for r in range(RANK // 8):
                    wbuf[2 * r + h, start + k] = out[8 * r : 8 * r + 8, 128 * k : 128 * k + 128]
            start += width

    def piece(buf, index):
        return buf.at[pl.ds(index * m, m)]

    def wat(q, xx):
        return wbuf.at[pl.ds((q * NX + xx) * m, m), pl.ds(0, nb)]

    def wlate(q, xx):
        return wbuf.at[pl.ds((q * NX + xx) * m, m), pl.ds(nb, na)]

    def wbundle(q):
        return wbuf.at[pl.ds(q * NX * m, NX * m), pl.ds(nb, na)]

    def slots(buf, index):
        return buf.at[pl.ds(index * NX * m, NX * m)]

    def add_into(ref, other):
        ref[...] = ref[...] + other[...]

    def stage_a(q, s):
        remote(wat(q, opp), piece(ropp, q), r_send.at[0], r_o.at[q], (to_right, to_left)[s]).start()

    def stage_b(q, s):
        wait(piece(ropp, q), r_o.at[q])
        add_into(wat(q, (right, left)[s]), piece(ropp, q))
        remote(wat(q, right), piece(rleft, q), r_send.at[0], r_l.at[q], to_right).start()
        remote(wat(q, left), piece(rright, q), r_send.at[0], r_r.at[q], to_left).start()

    def stage_c(q):
        wait(piece(rleft, q), r_l.at[q])
        wait(piece(rright, q), r_r.at[q])
        here = wat(q, x)
        here[...] = here[...] + (piece(rleft, q)[...] + piece(rright, q)[...])

    def z_sum(j, top, q, ref, place, odd, even, s_odd, s_even, to_one, to_two, up):
        def slot(last):
            return jnp.where(last, nz, q) if up else q

        is_odd = lax.rem(j, 2) == 1

        @pl.when(is_odd & (j <= top))
        def _():
            at = slot(j == 1)
            remote(ref, place(odd, at), r_send.at[0], s_odd.at[at], to_one).start()

        @pl.when(jnp.logical_not(is_odd) & (j >= 2) & (j <= top))
        def _():
            @pl.when(j + 1 <= top)
            def _():
                wait(place(odd, q), s_odd.at[q])
                add_into(ref, place(odd, q))

            @pl.when(j + 2 <= top)
            def _():
                wait(place(even, q), s_even.at[q])
                add_into(ref, place(even, q))

            at = slot(j == 2)
            remote(ref, place(even, at), r_send.at[0], s_even.at[at], to_two).start()

    def z_last(ref, place, odd, even, s_odd, s_even):
        for buf, sem, index, there in (
            (odd, s_odd, z, half >= 1), (even, s_even, z, half >= 2),
            (odd, s_odd, nz, half >= 2), (even, s_even, nz, half >= 3),
        ):
            if there:
                wait(place(buf, index), sem.at[index])
                add_into(ref, place(buf, index))

    def early_sum(j):
        args = (slots, aodd, aeven, a_odd, a_even)
        q = zmod(z - j)
        z_sum(j, half, q, wbundle(q), *args, to_down, to_down2, False)
        q = zmod(z + j)
        z_sum(j, half - 1, q, wbundle(q), *args, to_up, to_up2, True)

        @pl.when(j == 0)
        def _():
            z_last(wbundle(z), *args)
            for xx, device in ((left, to_left), (right, to_right), (opp, to_opp)):
                remote(wlate(z, xx), piece(across, x), r_send.at[0], a_odd.at[nz + 1], device).start()
            piece(across, x)[...] = wlate(z, x)[...]

    def late_sum(j):
        args = (piece, rodd, reven, r_odd, r_even)
        q = zmod(z - j)
        stage_c(q)
        z_sum(j, half, q, wat(q, x), *args, to_down, to_down2, False)

        @pl.when((j >= 1) & (j < half))
        def _():
            q = zmod(z + j)
            stage_c(q)
            z_sum(j, half - 1, q, wat(q, x), *args, to_up, to_up2, True)

        @pl.when(j == 0)
        def _():
            z_last(wat(z, x), *args)

    def reduce_step(i, carry):
        @pl.when(i <= half)
        def _():
            stage_a(zmod(z - half + i), 0)

        @pl.when((i >= 1) & (i < half))
        def _():
            stage_a(zmod(z + half - i), 1)

        b = i - 1

        @pl.when((b >= 0) & (b <= half))
        def _():
            stage_b(zmod(z - half + b), 0)

        @pl.when((b >= 1) & (b < half))
        def _():
            stage_b(zmod(z + half - b), 1)

        @pl.when(i <= half)
        def _():
            early_sum(half - i)

        @pl.when(i >= 2)
        def _():
            late_sum(half + 2 - i)

        @pl.when(i == max(1, half // 4))
        def _():
            gram_over_z()

        @pl.when(i == max(2, half // 2))
        def _():
            gram_over_x()

        @pl.when(i == max(3, 3 * half // 4))
        def _():
            gram_over_t()

        return carry

    lax.fori_loop(0, half + 3, reduce_step, 0)
    wait(across.at[pl.ds(0, (NX - 1) * m)], a_odd.at[nz + 1])
    wfin[pl.ds(f * m, m), 0:nb] = wat(z, x)[...]
    wfin[pl.ds(f * m, m), nb:] = jnp.sum(across[...].reshape(NX, m, na, 8, 128), axis=0)
    gram_done()

    lane = lax.broadcasted_iota(jnp.int32, (PANEL, 128), 1)
    down = lax.broadcasted_iota(jnp.int32, (PANEL, 128), 0)
    wide = lax.broadcasted_iota(jnp.int32, (PANEL, RANK), 1)
    npanel = RANK // PANEL

    def panel(b):
        here = pl.ds(pl.multiple_of(b * PANEL, PANEL), PANEL)
        block = elim[here, :]
        turned = pltpu.roll(block[:, :RANK], lax.rem(RANK - b * PANEL, RANK), 1)[:, :128]
        state = jnp.where(lane < PANEL, turned, jnp.where(lane == down + PANEL, 1.0, 0.0))
        for first in range(0, PANEL, MINI):
            spread = [
                jnp.broadcast_to(state[:, k : k + 1], (PANEL, 128)) for k in range(first, first + MINI)
            ]
            for k in range(min(MINI, PANEL - 1 - first)):
                j = first + k
                scale = jnp.where(down > j, spread[k], 0.0) * (1.0 / spread[k][j : j + 1, :])
                state = state - scale * state[j : j + 1, :]
                for n in range(k + 1, MINI):
                    spread[n] = spread[n] - scale * spread[n][j : j + 1, :]
        diag = jnp.sum(jnp.where(lane == down, state, 0.0), axis=1, keepdims=True)
        lower = state[:, PANEL : 2 * PANEL] / jnp.sqrt(diag)
        done = dot_full(lower, block, NN)
        rest = jnp.where(wide >= (b + 1) * PANEL, done[:, :RANK], 0.0)
        (rh, rm, rl), (dh, dm, dl) = split3(rest), split3(done)
        elim[...] = elim[...] - dot(
            jnp.concatenate([rh, rh, rh, rm, rm, rl], axis=0),
            jnp.concatenate([dh, dm, dl, dh, dm, dh], axis=0),
            TN,
        )
        elim[here, :] = done

    def panels(j):
        for k in range(npanel // half):
            panel((j - 1) * (npanel // half) + k)

    gather(wfin, nb, w_send.at[0], w_z, w_l, w_r, w_o, w_a, lambda: None, panels)
    wait(wbuf.at[pl.ds(0, (nz * NX - 1) * m)], r_send.at[0])

    inv_lower = elim[:, RANK:]
    ortho = dot_full(proj[...], inv_lower, NT)
    low = split(inv_lower)
    squared = jnp.zeros((RANK, 128), F32)
    cuts = []
    for h in range(2):
        start = 0
        while start < nh:
            width = min(4, nh - start) if nh - start != 5 else 5
            cuts.append((h, start, width))
            start += width
    for h, start, width in cuts:
        cut = slice((h * nh + start) * 128, (h * nh + start + width) * 128)
        columns = [
            jnp.concatenate([wfin[2 * r + h, start + k] for r in range(RANK // 8)], axis=0)
            for k in range(width)
        ]
        out = dot3(low, split(jnp.concatenate(columns, axis=1)), NN)
        for k in range(width):
            one = out[:, 128 * k : 128 * k + 128]
            squared = squared + one * one
        rhi[:, cut], rlo[:, cut] = split(out)
    nbuf[t] = dot_full(jnp.ones((8, 128), F32), squared, NT)

    if nt > 1:
        def send_norm(r, carry):
            remote(
                nbuf.at[t], nbuf.at[t], s_send.at[6], s_recv.at[6], (f, tmod(t + r))
            ).start()
            return carry

        lax.fori_loop(1, nt, send_norm, 0)

    ortho_high = ortho.astype(BF16)
    stores = []
    for n, (h, start, width) in enumerate(cuts):
        cut = slice((h * nh + start) * 128, (h * nh + start + width) * 128)
        mom[:, cut] = mom[:, cut] - 0.05 * dot(ortho_high, rhi[:, cut], NN)
        stores.append(pltpu.make_async_copy(mom.at[:, cut], newm_hbm.at[:, cut], store_sem.at[n]))
        stores[-1].start()

    if nt > 1:
        wait(nbuf.at[pl.ds(0, nt - 1)], s_recv.at[6])
        wait(nbuf.at[pl.ds(0, nt - 1)], s_send.at[6])
    norm = nbuf[0]
    for r in range(1, nt):
        norm = norm + nbuf[r]
    inverse = 1.0 / (jnp.sqrt(norm) + 1e-06)
    scaled = split(ortho * (inverse[0:1, :] * -factor))
    for n, (h, start, width) in enumerate(cuts):
        cut = slice((h * nh + start) * 128, (h * nh + start + width) * 128)
        dout[:, cut] = dot3(scaled, (rhi[:, cut], rlo[:, cut]), NN).astype(BF16)
        stores.append(
            pltpu.make_async_copy(dout.at[:, cut], delta_hbm.at[:, cut], store_sem.at[len(cuts) + n])
        )
        stores[-1].start()
    for store in stores:
        store.wait()


def per_device(nz, nt, factor, momentum, gradient, basis):
    rows, cols = momentum.shape
    nblk = cols // 128
    nh = nblk // 2
    m = GROUPS // (nz * NX)
    gshare = RANK // nt
    ng = 2 * gshare // 4
    mg = ng // nz
    na = max(1, nh // 4)
    nb = nh - na
    tiles = basis.reshape(m, 4, nblk, 128).transpose(0, 2, 1, 3)
    vmem = pltpu.VMEM
    dma = pltpu.SemaphoreType.DMA
    any_spec = pl.BlockSpec(memory_space=pl.ANY)
    one = max(nt - 1, 1)
    return pl.pallas_call(
        functools.partial(kernel, nz, nt, factor),
        out_shape=(
            jax.ShapeDtypeStruct((rows, cols), F32),
            jax.ShapeDtypeStruct((rows, cols), BF16),
        ),
        in_specs=[any_spec] * 3,
        out_specs=(any_spec, any_spec),
        scratch_shapes=[
            vmem((rows, cols), F32),
            vmem((rows, cols), BF16),
            vmem((rows, cols), BF16),
            vmem((rows, cols), BF16),
            vmem((GROUPS, nblk, 4, 128), F32),
            vmem((rows, RANK), F32),
            vmem((rows, RANK), F32),
            vmem((one, rows // nt, RANK), F32),
            vmem((GROUPS, nh, 8, 128), F32),
            vmem((nz * m, nb, 8, 128), F32),
            vmem((nz * m, nb, 8, 128), F32),
            vmem((nz * m, nb, 8, 128), F32),
            vmem(((nz + 1) * m, nb, 8, 128), F32),
            vmem(((nz + 1) * m, nb, 8, 128), F32),
            vmem(((nz + 1) * NX * m, na, 8, 128), F32),
            vmem(((nz + 1) * NX * m, na, 8, 128), F32),
            vmem((NX * m, na, 8, 128), F32),
            vmem((GROUPS, nh, 8, 128), F32),
            vmem((RANK, RANK), F32),
            vmem((ng, 4, 128), F32),
            vmem((nz - 1, mg, 4, 128), F32),
            vmem((mg, 4, 128), F32),
            vmem((NX, mg, 4, 128), F32),
            vmem((2 * GROUPS, 4, 128), F32),
            vmem((RANK, 2 * RANK), F32),
            vmem((RANK, cols), BF16),
            vmem((RANK, cols), BF16),
            vmem((nt, 8, RANK), F32),
            vmem((rows, cols), BF16),
            dma((3,)),
            dma((16,)),
            dma((1,)), dma((nz,)), dma((nz,)), dma((nz,)), dma((nz,)), dma((nz + 1,)),
            dma((1,)), dma((nz,)), dma((nz,)), dma((nz,)), dma((nz,)), dma((nz + 1,)),
            dma((1,)), dma((nz + 1,)), dma((nz + 1,)), dma((nz + 2,)), dma((nz + 1,)),
            dma((nz,)), dma((nz,)), dma((nz,)),
            dma((7,)),
            dma((7,)),
        ],
        compiler_params=pltpu.CompilerParams(
            collective_id=0, has_side_effects=True, vmem_limit_bytes=56 * 2**20
        ),
        name="dion_step",
    )(momentum, gradient, tiles)


def solution(mesh):
    nz, nt = mesh.shape["fsdp"] // NX, mesh.shape["tensor"]
    factor = (ROWS * COLS / RANK) ** 0.5
    spec = P("fsdp", "tensor")
    return jax.shard_map(
        functools.partial(per_device, nz, nt, factor),
        mesh=mesh, in_specs=(spec,) * 3, out_specs=(spec,) * 2, check_vma=False,
    )
```

```python
import functools

import jax
import jax.numpy as jnp
from jax import lax
from jax.experimental import pallas as pl
from jax.experimental.pallas import tpu as pltpu
from jax.sharding import PartitionSpec as P

ROWS = 8192
COLS = 26624
RANK = 256
NX = 4
GROUPS = RANK // 4
PANEL = 32
MINI = 16
NA = 2
LAG = 2
LAG_B = 2
LAG_C = 4
GRAM_AT = (2, 4, 6, 9)
F32 = jnp.float32
BF16 = jnp.bfloat16
HIGHEST = lax.Precision.HIGHEST
NT = (((1,), (1,)), ((), ()))
TN = (((0,), (0,)), ((), ()))
NN = (((1,), (0,)), ((), ()))


def split3(value):
    high = value.astype(BF16)
    rest = value - high.astype(F32)
    mid = rest.astype(BF16)
    return high, mid, (rest - mid.astype(F32)).astype(BF16)


def split(value):
    high = value.astype(BF16)
    return high, (value - high.astype(F32)).astype(BF16)


def dot(a, b, dims):
    return lax.dot_general(a, b, dims, preferred_element_type=F32)


def dot3(a, b, dims):
    (ah, al), (bh, bl) = a, b
    return dot(ah, bh, dims) + (dot(ah, bl, dims) + dot(al, bh, dims))


def dot_full(a, b, dims):
    return lax.dot_general(a, b, dims, precision=HIGHEST, preferred_element_type=F32)


def cuts_of(nh):
    cuts = []
    for h in range(2):
        start = 0
        while start < nh:
            width = min(4, nh - start) if nh - start != 5 else 5
            cuts.append((h, start, width))
            start += width
    return cuts


def kernel(
    nz, nt, factor,
    mom_hbm, grad_hbm, basis_hbm, high_hbm, low_hbm, ortho_out, scaled_high, scaled_low,
    mom, grad, bhi, blo, vbuf, part, proj, rsbuf,
    wbuf, ropp, rleft, rright, rodd, reven, aodd, aeven, across, wfin,
    gram, gslice, grs, gsum, gx, gall, elim,
    rhi, rlo, nbuf,
    load_sem, store_sem, v_send, v_z, v_l, v_r, v_o, v_a,
    w_send, w_z, w_l, w_r, w_o, w_a, r_send, r_odd, r_even, a_odd, a_even, r_l, r_r, r_o,
    s_send, s_recv,
):
    rows, cols = mom.shape
    nblk = cols // 128
    nh = nblk // 2
    half = nz // 2
    na = across.shape[1]
    nb = nh - na
    m = GROUPS // (nz * NX)
    f = lax.axis_index("fsdp")
    t = lax.axis_index("tensor")
    z, x = lax.div(f, NX), lax.rem(f, NX)
    left, right, opp = lax.rem(x + NX - 1, NX), lax.rem(x + 1, NX), lax.rem(x + 2, NX)

    def zmod(value):
        return lax.rem(value + nz, nz)

    def tmod(value):
        return lax.rem(value + nt, nt)

    def dev(zz, xx):
        return (zz * NX + xx, t)

    to_up, to_down = dev(zmod(z + 1), x), dev(zmod(z - 1), x)
    to_up2, to_down2 = dev(zmod(z + 2), x), dev(zmod(z - 2 + nz), x)
    to_left, to_right, to_opp = dev(z, left), dev(z, right), dev(z, opp)

    def remote(src, dst, send, recv, device):
        return pltpu.make_async_remote_copy(
            src_ref=src, dst_ref=dst, send_sem=send, recv_sem=recv,
            device_id=device, device_id_type=pl.DeviceIdType.MESH,
        )

    def wait(ref, sem):
        pltpu.make_async_copy(ref, ref, sem).wait()

    load_basis = pltpu.make_async_copy(basis_hbm, vbuf.at[pl.ds(f * m, m)], load_sem.at[0])
    load_mom = pltpu.make_async_copy(mom_hbm, mom, load_sem.at[1])
    load_grad = pltpu.make_async_copy(grad_hbm, grad, load_sem.at[2])
    load_basis.start()
    load_mom.start()
    load_grad.start()

    barrier = pltpu.get_barrier_semaphore()

    def greet(device):
        pl.semaphore_signal(barrier, inc=1, device_id=device, device_id_type=pl.DeviceIdType.MESH)

    def greet_t(r, carry):
        greet((f, tmod(t + r)))
        return carry

    lax.fori_loop(1, nt, greet_t, 0)
    near = [to_left, to_right, to_opp]
    near += [dev(zmod(z + r), x) for r in sorted({1 % nz, nz - 1, 2 % nz, nz - 2} - {0})]
    for device in near:
        greet(device)
    pl.semaphore_wait(barrier, (nt - 1) + len(near))

    def gather(buf, cut, send, sz, sl, sr, so, sa, early, hook):
        whole = buf.shape[1]

        def at(zz, xx):
            return buf.at[pl.ds((zz * NX + xx) * m, m), pl.ds(0, cut)]

        def late(zz, xx):
            return buf.at[pl.ds((zz * NX + xx) * m, m), pl.ds(cut, whole - cut)]

        def bundle(zz):
            return buf.at[pl.ds(zz * NX * m, NX * m), pl.ds(cut, whole - cut)]

        def onward(j, ref, sem):
            @pl.when(j + 2 <= half)
            def _():
                remote(ref, ref, send, sem, to_up2).start()

            @pl.when(j + 1 <= half)
            def _():
                remote(ref, ref, send, sem, to_up).start()

        def back(j, ref, sem):
            @pl.when(j + 2 < half)
            def _():
                remote(ref, ref, send, sem, to_down2).start()

            @pl.when(j + 1 < half)
            def _():
                remote(ref, ref, send, sem, to_down).start()

        def push(zz, xx, sem, device):
            remote(at(zz, xx), at(zz, xx), send, sem.at[zz], device).start()

        def spread(zz):
            push(zz, x, sl, to_right)
            push(zz, x, sr, to_left)

        def pass_right(zz):
            wait(at(zz, left), sl.at[zz])
            push(zz, left, so, to_right)

        def pass_left(zz):
            wait(at(zz, right), sr.at[zz])
            push(zz, right, so, to_left)

        def passing(j):
            @pl.when(j >= 0)
            def _():
                pass_right(zmod(z - j))

            @pl.when((j > 0) & (j < half))
            def _():
                pass_left(zmod(z + j))

        for device in (to_right, to_left, to_opp):
            remote(late(z, x), late(z, x), send, sa.at[nz], device).start()
        onward(0, at(z, x), sz.at[z])
        back(0, at(z, x), sz.at[z])
        spread(z)
        early()
        wait(buf.at[pl.ds(0, (NX - 1) * m), pl.ds(cut, whole - cut)], sa.at[nz])
        onward(0, bundle(z), sa.at[z])
        back(0, bundle(z), sa.at[z])

        def step(j, carry):
            below, above = zmod(z - j), zmod(z + j)
            even = lax.rem(j, 2) == 0
            def late_ones():
                wait(bundle(below), sa.at[below])

                @pl.when(even)
                def _():
                    onward(j, bundle(below), sa.at[below])

                @pl.when(j < half)
                def _():
                    wait(bundle(above), sa.at[above])

                    @pl.when(even)
                    def _():
                        back(j, bundle(above), sa.at[above])

            wait(at(below, x), sz.at[below])

            @pl.when(even)
            def _():
                onward(j, at(below, x), sz.at[below])

            @pl.when(j < half)
            def _():
                wait(at(above, x), sz.at[above])

                @pl.when(even)
                def _():
                    back(j, at(above, x), sz.at[above])

            spread(below)

            @pl.when(j < half)
            def _():
                spread(above)

            late_ones()
            passing(j - LAG)
            hook(j)
            return carry

        lax.fori_loop(1, half + 1, step, 0)
        lax.fori_loop(half + 1 - LAG, half + 1, lambda j, carry: (passing(j), carry)[1], 0)

        def finish(j, carry):
            below, above = zmod(z - j), zmod(z + j)
            wait(at(below, right), sr.at[below])
            wait(at(below, opp), so.at[below])

            @pl.when((j > 0) & (j < half))
            def _():
                wait(at(above, left), sl.at[above])
                wait(at(above, opp), so.at[above])

            return carry

        lax.fori_loop(0, half + 1, finish, 0)
        wait(buf.at[pl.ds(0, (nz * NX - 1) * m)], send)

    load_basis.wait()

    def make_blend():
        load_mom.wait()
        load_grad.wait()

        def body(c, carry):
            cut = pl.ds(pl.multiple_of(c * 256, 256), 256)
            blend = mom[:, cut] + grad[:, cut].astype(F32)
            mom[:, cut] = blend
            bhi[:, cut], blo[:, cut] = split(blend)
            return carry

        lax.fori_loop(0, nblk // 2, body, 0)

    gather(vbuf, 2 * nb, v_send.at[0], v_z, v_l, v_r, v_o, v_a, make_blend, lambda j: None)

    def project(c, acc):
        cut = pl.ds(pl.multiple_of(c * 256, 256), 256)
        pair = [vbuf[:, 2 * c + k].reshape(RANK, 128) for k in range(2)]
        return acc + dot3((bhi[:, cut], blo[:, cut]), split(jnp.concatenate(pair, axis=1)), NT)

    part[...] = lax.fori_loop(0, nblk // 2, project, jnp.zeros((rows, RANK), F32))

    share = rows // nt
    if nt > 1:
        own = pl.ds(t * share, share)

        def send_part(r, carry):
            peer = tmod(t + r)
            remote(
                part.at[pl.ds(peer * share, share)], rsbuf.at[r - 1],
                s_send.at[0], s_recv.at[0], (f, peer),
            ).start()
            return carry

        lax.fori_loop(1, nt, send_part, 0)
        wait(rsbuf, s_recv.at[0])
        total = part[own]
        for r in range(nt - 1):
            total = total + rsbuf[r]
        proj[own] = total

        def send_sum(r, carry):
            remote(
                proj.at[own], proj.at[own], s_send.at[1], s_recv.at[1], (f, tmod(t + r))
            ).start()
            return carry

        lax.fori_loop(1, nt, send_sum, 0)
        wait(proj.at[pl.ds(0, (nt - 1) * share)], s_recv.at[1])
        wait(rsbuf, s_send.at[0])
        wait(proj.at[pl.ds(0, (nt - 1) * share)], s_send.at[1])
    else:
        proj[...] = part[...]

    full = proj[...]
    gram[...] = dot_full(full, full, TN)
    gshare = RANK // nt
    ng = 2 * gshare // 4
    mg = ng // nz
    mine = gram[pl.ds(t * gshare, gshare), :]
    for r in range(gshare // 4):
        for c in range(2):
            gslice[2 * r + c] = mine[4 * r : 4 * r + 4, 128 * c : 128 * c + 128]

    def gram_send():
        def body(r, carry):
            peer = zmod(z + r)
            remote(
                gslice.at[pl.ds(peer * mg, mg)], grs.at[r - 1],
                s_send.at[2], s_recv.at[2], dev(peer, x),
            ).start()
            return carry

        lax.fori_loop(1, nz, body, 0)

    def gram_over_z():
        wait(grs, s_recv.at[2])
        gsum[...] = gslice[pl.ds(z * mg, mg)] + jnp.sum(grs[...], axis=0)
        gx[x] = gsum[...]
        for k, device in enumerate((to_left, to_right, to_opp)):
            remote(gsum, gx.at[x], s_send.at[3], s_recv.at[3], device).start()

    def gram_over_x():
        wait(gx.at[pl.ds(0, NX - 1)], s_recv.at[3])
        here = pl.ds(t * ng + z * mg, mg)
        gall[here] = jnp.sum(gx[...], axis=0)

        def body(r, carry):
            remote(
                gall.at[here], gall.at[here], s_send.at[4], s_recv.at[4], dev(zmod(z + r), x)
            ).start()
            return carry

        lax.fori_loop(1, nz, body, 0)

    def gram_over_t():
        wait(gall.at[pl.ds(0, (nz - 1) * mg)], s_recv.at[4])
        if nt > 1:
            here = pl.ds(t * ng, ng)

            def body(r, carry):
                remote(
                    gall.at[here], gall.at[here], s_send.at[5], s_recv.at[5], (f, tmod(t + r))
                ).start()
                return carry

            lax.fori_loop(1, nt, body, 0)

    def gram_done():
        if nt > 1:
            wait(gall.at[pl.ds(0, (nt - 1) * ng)], s_recv.at[5])
            wait(gall.at[pl.ds(0, (nt - 1) * ng)], s_send.at[5])
        wait(grs, s_send.at[2])
        wait(gx.at[pl.ds(0, NX - 1)], s_send.at[3])
        wait(gall.at[pl.ds(0, (nz - 1) * mg)], s_send.at[4])
        for r in range(RANK // 8):
            for c in range(2):
                pair = [gall[4 * r + c], gall[4 * r + 2 + c]]
                elim[8 * r : 8 * r + 8, 128 * c : 128 * c + 128] = jnp.concatenate(pair, axis=0)
        down = lax.broadcasted_iota(jnp.int32, (RANK, RANK), 0)
        across = lax.broadcasted_iota(jnp.int32, (RANK, RANK), 1)
        elim[:, RANK:] = jnp.where(down == across, 1.0, 0.0).astype(F32)

    gram_send()

    turned = split(full.T)
    for h, start, width in cuts_of(nh):
        cut = slice((h * nh + start) * 128, (h * nh + start + width) * 128)
        out = dot3(turned, (bhi[:, cut], blo[:, cut]), NN)
        for k in range(width):
            for r in range(RANK // 8):
                wbuf[2 * r + h, start + k] = out[8 * r : 8 * r + 8, 128 * k : 128 * k + 128]

    def piece(buf, index):
        return buf.at[pl.ds(index * m, m)]

    def wat(q, xx):
        return wbuf.at[pl.ds((q * NX + xx) * m, m), pl.ds(0, nb)]

    def wlate(q, xx):
        return wbuf.at[pl.ds((q * NX + xx) * m, m), pl.ds(nb, na)]

    def wbundle(q):
        return wbuf.at[pl.ds(q * NX * m, NX * m), pl.ds(nb, na)]

    def slots(buf, index):
        return buf.at[pl.ds(index * NX * m, NX * m)]

    def add_into(ref, other):
        ref[...] = ref[...] + other[...]

    def stage_a(q, s):
        remote(wat(q, opp), piece(ropp, q), r_send.at[0], r_o.at[q], (to_right, to_left)[s]).start()

    def stage_b(q, s):
        wait(piece(ropp, q), r_o.at[q])
        add_into(wat(q, (right, left)[s]), piece(ropp, q))
        remote(wat(q, right), piece(rleft, q), r_send.at[0], r_l.at[q], to_right).start()
        remote(wat(q, left), piece(rright, q), r_send.at[0], r_r.at[q], to_left).start()

    def stage_c(q):
        wait(piece(rleft, q), r_l.at[q])
        wait(piece(rright, q), r_r.at[q])
        here = wat(q, x)
        here[...] = here[...] + (piece(rleft, q)[...] + piece(rright, q)[...])

    def z_sum(j, top, q, ref, place, odd, even, s_odd, s_even, to_one, to_two, up):
        def slot(last):
            return jnp.where(last, nz, q) if up else q

        is_odd = lax.rem(j, 2) == 1

        @pl.when(is_odd & (j <= top))
        def _():
            at = slot(j == 1)
            remote(ref, place(odd, at), r_send.at[0], s_odd.at[at], to_one).start()

        @pl.when(jnp.logical_not(is_odd) & (j >= 2) & (j <= top))
        def _():
            @pl.when(j + 1 <= top)
            def _():
                wait(place(odd, q), s_odd.at[q])
                add_into(ref, place(odd, q))

            @pl.when(j + 2 <= top)
            def _():
                wait(place(even, q), s_even.at[q])
                add_into(ref, place(even, q))

            at = slot(j == 2)
            remote(ref, place(even, at), r_send.at[0], s_even.at[at], to_two).start()

    def z_last(ref, place, odd, even, s_odd, s_even):
        for buf, sem, index, there in (
            (odd, s_odd, z, half >= 1), (even, s_even, z, half >= 2),
            (odd, s_odd, nz, half >= 2), (even, s_even, nz, half >= 3),
        ):
            if there:
                wait(place(buf, index), sem.at[index])
                add_into(ref, place(buf, index))

    def early_sum(j):
        args = (slots, aodd, aeven, a_odd, a_even)
        q = zmod(z - j)
        z_sum(j, half, q, wbundle(q), *args, to_down, to_down2, False)
        q = zmod(z + j)
        z_sum(j, half - 1, q, wbundle(q), *args, to_up, to_up2, True)

        @pl.when(j == 0)
        def _():
            z_last(wbundle(z), *args)
            for xx, device in ((left, to_left), (right, to_right), (opp, to_opp)):
                remote(wlate(z, xx), piece(across, x), r_send.at[0], a_odd.at[nz + 1], device).start()
            piece(across, x)[...] = wlate(z, x)[...]

    def late_sum(j):
        args = (piece, rodd, reven, r_odd, r_even)
        q = zmod(z - j)
        stage_c(q)
        z_sum(j, half, q, wat(q, x), *args, to_down, to_down2, False)

        @pl.when((j >= 1) & (j < half))
        def _():
            q = zmod(z + j)
            stage_c(q)
            z_sum(j, half - 1, q, wat(q, x), *args, to_up, to_up2, True)

        @pl.when(j == 0)
        def _():
            z_last(wat(z, x), *args)

    lane = lax.broadcasted_iota(jnp.int32, (PANEL, 128), 1)
    down = lax.broadcasted_iota(jnp.int32, (PANEL, 128), 0)
    wide = lax.broadcasted_iota(jnp.int32, (PANEL, RANK), 1)
    npanel = RANK // PANEL

    def panel(b):
        here = pl.ds(pl.multiple_of(b * PANEL, PANEL), PANEL)
        block = elim[here, :]
        turned = pltpu.roll(block[:, :RANK], lax.rem(RANK - b * PANEL, RANK), 1)[:, :128]
        state = jnp.where(lane < PANEL, turned, jnp.where(lane == down + PANEL, 1.0, 0.0))
        for first in range(0, PANEL, MINI):
            spread = [
                jnp.broadcast_to(state[:, k : k + 1], (PANEL, 128)) for k in range(first, first + MINI)
            ]
            for k in range(min(MINI, PANEL - 1 - first)):
                j = first + k
                scale = jnp.where(down > j, spread[k], 0.0) * (1.0 / spread[k][j : j + 1, :])
                state = state - scale * state[j : j + 1, :]
                for n in range(k + 1, MINI):
                    spread[n] = spread[n] - scale * spread[n][j : j + 1, :]
        diag = jnp.sum(jnp.where(lane == down, state, 0.0), axis=1, keepdims=True)
        lower = state[:, PANEL : 2 * PANEL] / jnp.sqrt(diag)
        done = dot_full(lower, block, NN)
        rest = jnp.where(wide >= (b + 1) * PANEL, done[:, :RANK], 0.0)
        (rh, rm, rl), (dh, dm, dl) = split3(rest), split3(done)
        elim[...] = elim[...] - dot(
            jnp.concatenate([rh, rh, rh, rm, rm, rl], axis=0),
            jnp.concatenate([dh, dm, dl, dh, dm, dh], axis=0),
            TN,
        )
        elim[here, :] = done

    def reduce_step(i, carry):
        @pl.when(i <= half)
        def _():
            stage_a(zmod(z - half + i), 0)

        @pl.when((i >= 1) & (i < half))
        def _():
            stage_a(zmod(z + half - i), 1)

        b = i - LAG_B

        @pl.when((b >= 0) & (b <= half))
        def _():
            stage_b(zmod(z - half + b), 0)

        @pl.when((b >= 1) & (b < half))
        def _():
            stage_b(zmod(z + half - b), 1)

        @pl.when(i <= half)
        def _():
            early_sum(half - i)

        @pl.when(i >= LAG_C)
        def _():
            late_sum(half + LAG_C - i)

        last = half + LAG_C
        for place, work in zip(GRAM_AT, (gram_over_z, gram_over_x, gram_over_t, gram_done)):
            pl.when(i == min(place, last))(work)

        @pl.when(i > max(GRAM_AT))
        def _():
            panel(i - max(GRAM_AT) - 1)

        return carry

    lax.fori_loop(0, half + 1 + LAG_C, reduce_step, 0)
    wait(across.at[pl.ds(0, (NX - 1) * m)], a_odd.at[nz + 1])
    wfin[pl.ds(f * m, m), 0:nb] = wat(z, x)[...]
    wfin[pl.ds(f * m, m), nb:] = jnp.sum(across[...].reshape(NX, m, na, 8, 128), axis=0)

    begun = max(0, half + LAG_C - max(GRAM_AT))

    def panels(j):
        for k in range(-(-(npanel - begun) // half)):
            b = begun + (j - 1) * (-(-(npanel - begun) // half)) + k
            pl.when(b < npanel)(functools.partial(panel, b))

    gather(wfin, nb, w_send.at[0], w_z, w_l, w_r, w_o, w_a, lambda: None, panels)
    wait(wbuf.at[pl.ds(0, (nz * NX - 1) * m)], r_send.at[0])

    inv_lower = elim[:, RANK:]
    ortho = dot_full(proj[...], inv_lower, NT)
    low = split(inv_lower)
    squared = jnp.zeros((RANK, 128), F32)
    stores = []
    for n, (h, start, width) in enumerate(cuts_of(nh)):
        cut = slice((h * nh + start) * 128, (h * nh + start + width) * 128)
        columns = [
            jnp.concatenate([wfin[2 * r + h, start + k] for r in range(RANK // 8)], axis=0)
            for k in range(width)
        ]
        out = dot3(low, split(jnp.concatenate(columns, axis=1)), NN)
        for k in range(width):
            one = out[:, 128 * k : 128 * k + 128]
            squared = squared + one * one
        rhi[:, cut], rlo[:, cut] = split(out)
        for k, (buf, hbm) in enumerate(((rhi, high_hbm), (rlo, low_hbm))):
            stores.append(pltpu.make_async_copy(buf.at[:, cut], hbm.at[:, cut], store_sem.at[2 * n + k]))
            stores[-1].start()
    nbuf[t] = dot_full(jnp.ones((8, 128), F32), squared, NT)

    if nt > 1:
        def send_norm(r, carry):
            remote(
                nbuf.at[t], nbuf.at[t], s_send.at[6], s_recv.at[6], (f, tmod(t + r))
            ).start()
            return carry

        lax.fori_loop(1, nt, send_norm, 0)

    ortho_out[...] = ortho.astype(BF16)
    if nt > 1:
        wait(nbuf.at[pl.ds(0, nt - 1)], s_recv.at[6])
        wait(nbuf.at[pl.ds(0, nt - 1)], s_send.at[6])
    norm = nbuf[0]
    for r in range(1, nt):
        norm = norm + nbuf[r]
    inverse = 1.0 / (jnp.sqrt(norm) + 1e-06)
    scaled_high[...], scaled_low[...] = split(ortho * (inverse[0:1, :] * -factor))
    for store in stores:
        store.wait()


def update(
    mom_hbm, grad_hbm, high_hbm, low_hbm, ortho, scaled_high, scaled_low, newm_hbm, delta_hbm,
    mom, grad, rhi, rlo, dout, load_sem, store_sem,
):
    cuts = cuts_of(mom.shape[1] // 256)
    nh = mom.shape[1] // 256
    pairs = ((high_hbm, rhi), (low_hbm, rlo), (mom_hbm, mom), (grad_hbm, grad))
    loads, stores = [], []
    for n, (h, start, width) in enumerate(cuts):
        cut = slice((h * nh + start) * 128, (h * nh + start + width) * 128)
        for k, (hbm, buf) in enumerate(pairs):
            loads.append(pltpu.make_async_copy(hbm.at[:, cut], buf.at[:, cut], load_sem.at[4 * n + k]))
            loads[-1].start()
    both = jnp.concatenate([scaled_high[...], scaled_low[...], ortho[...]], axis=0)
    rows = ortho.shape[0]
    for n, (h, start, width) in enumerate(cuts):
        cut = slice((h * nh + start) * 128, (h * nh + start + width) * 128)
        for load in loads[4 * n : 4 * n + 4]:
            load.wait()
        high = dot(both, rhi[:, cut], NN)
        delta = high[:rows] + (high[rows : 2 * rows] + dot(scaled_high[...], rlo[:, cut], NN))
        dout[:, cut] = delta.astype(BF16)
        mom[:, cut] = (mom[:, cut] + grad[:, cut].astype(F32)) - 0.05 * high[2 * rows :]
        for k, (buf, hbm) in enumerate(((mom, newm_hbm), (dout, delta_hbm))):
            stores.append(pltpu.make_async_copy(buf.at[:, cut], hbm.at[:, cut], store_sem.at[2 * n + k]))
            stores[-1].start()
    for store in stores:
        store.wait()


def per_device(nz, nt, factor, momentum, gradient, basis):
    rows, cols = momentum.shape
    nblk = cols // 128
    nh = nblk // 2
    m = GROUPS // (nz * NX)
    gshare = RANK // nt
    ng = 2 * gshare // 4
    mg = ng // nz
    na = min(NA, nh - 1)
    nb = nh - na
    tiles = basis.reshape(m, 4, nblk, 128).transpose(0, 2, 1, 3)
    vmem = pltpu.VMEM
    dma = pltpu.SemaphoreType.DMA
    any_spec = pl.BlockSpec(memory_space=pl.ANY)
    one = max(nt - 1, 1)
    vmem_spec = pl.BlockSpec(memory_space=pltpu.VMEM)
    ncut = len(cuts_of(nh))
    high, low, ortho, scaled_high, scaled_low = pl.pallas_call(
        functools.partial(kernel, nz, nt, factor),
        out_shape=(
            jax.ShapeDtypeStruct((RANK, cols), BF16),
            jax.ShapeDtypeStruct((RANK, cols), BF16),
            jax.ShapeDtypeStruct((rows, RANK), BF16),
            jax.ShapeDtypeStruct((rows, RANK), BF16),
            jax.ShapeDtypeStruct((rows, RANK), BF16),
        ),
        in_specs=[any_spec] * 3,
        out_specs=(any_spec, any_spec, vmem_spec, vmem_spec, vmem_spec),
        scratch_shapes=[
            vmem((rows, cols), F32),
            vmem((rows, cols), BF16),
            vmem((rows, cols), BF16),
            vmem((rows, cols), BF16),
            vmem((GROUPS, nblk, 4, 128), F32),
            vmem((rows, RANK), F32),
            vmem((rows, RANK), F32),
            vmem((one, rows // nt, RANK), F32),
            vmem((GROUPS, nh, 8, 128), F32),
            vmem((nz * m, nb, 8, 128), F32),
            vmem((nz * m, nb, 8, 128), F32),
            vmem((nz * m, nb, 8, 128), F32),
            vmem(((nz + 1) * m, nb, 8, 128), F32),
            vmem(((nz + 1) * m, nb, 8, 128), F32),
            vmem(((nz + 1) * NX * m, na, 8, 128), F32),
            vmem(((nz + 1) * NX * m, na, 8, 128), F32),
            vmem((NX * m, na, 8, 128), F32),
            vmem((GROUPS, nh, 8, 128), F32),
            vmem((RANK, RANK), F32),
            vmem((ng, 4, 128), F32),
            vmem((nz - 1, mg, 4, 128), F32),
            vmem((mg, 4, 128), F32),
            vmem((NX, mg, 4, 128), F32),
            vmem((2 * GROUPS, 4, 128), F32),
            vmem((RANK, 2 * RANK), F32),
            vmem((RANK, cols), BF16),
            vmem((RANK, cols), BF16),
            vmem((nt, 8, RANK), F32),
            dma((3,)),
            dma((2 * ncut,)),
            dma((1,)), dma((nz,)), dma((nz,)), dma((nz,)), dma((nz,)), dma((nz + 1,)),
            dma((1,)), dma((nz,)), dma((nz,)), dma((nz,)), dma((nz,)), dma((nz + 1,)),
            dma((1,)), dma((nz + 1,)), dma((nz + 1,)), dma((nz + 2,)), dma((nz + 1,)),
            dma((nz,)), dma((nz,)), dma((nz,)),
            dma((7,)),
            dma((7,)),
        ],
        compiler_params=pltpu.CompilerParams(
            collective_id=0, has_side_effects=True, vmem_limit_bytes=56 * 2**20
        ),
        name="dion_step",
    )(momentum, gradient, tiles)
    return pl.pallas_call(
        update,
        out_shape=(
            jax.ShapeDtypeStruct((rows, cols), F32),
            jax.ShapeDtypeStruct((rows, cols), BF16),
        ),
        in_specs=[any_spec] * 4 + [vmem_spec] * 3,
        out_specs=(any_spec, any_spec),
        scratch_shapes=[
            vmem((rows, cols), F32),
            vmem((rows, cols), BF16),
            vmem((RANK, cols), BF16),
            vmem((RANK, cols), BF16),
            vmem((rows, cols), BF16),
            dma((4 * ncut,)),
            dma((2 * ncut,)),
        ],
        compiler_params=pltpu.CompilerParams(vmem_limit_bytes=56 * 2**20),
        name="dion_update",
    )(momentum, gradient, high, low, ortho, scaled_high, scaled_low)


def solution(mesh):
    nz, nt = mesh.shape["fsdp"] // NX, mesh.shape["tensor"]
    factor = (ROWS * COLS / RANK) ** 0.5
    spec = P("fsdp", "tensor")
    return jax.shard_map(
        functools.partial(per_device, nz, nt, factor),
        mesh=mesh, in_specs=(spec,) * 3, out_specs=(spec,) * 2, check_vma=False,
    )
```

```python
import functools

import jax
import jax.numpy as jnp
from jax import lax
from jax.experimental import pallas as pl
from jax.experimental.pallas import tpu as pltpu
from jax.sharding import PartitionSpec as P

ROWS = 8192
COLS = 26624
RANK = 256
NX = 4
GROUPS = RANK // 4
PANEL = 32
MINI = 16
NA = 2
LAG = 2
LAG_A = 2
UNROLL = 13
LAG_S = 1
LAG_B = 2
LAG_C = 4
GRAM_AT = (2, 4, 6, 9)
F32 = jnp.float32
BF16 = jnp.bfloat16
HIGHEST = lax.Precision.HIGHEST
NT = (((1,), (1,)), ((), ()))
TN = (((0,), (0,)), ((), ()))
NN = (((1,), (0,)), ((), ()))


def split3(value):
    high = value.astype(BF16)
    rest = value - high.astype(F32)
    mid = rest.astype(BF16)
    return high, mid, (rest - mid.astype(F32)).astype(BF16)


def split(value):
    high = value.astype(BF16)
    return high, (value - high.astype(F32)).astype(BF16)


def dot(a, b, dims):
    return lax.dot_general(a, b, dims, preferred_element_type=F32)


def dot3(a, b, dims):
    (ah, al), (bh, bl) = a, b
    return dot(ah, bh, dims) + (dot(ah, bl, dims) + dot(al, bh, dims))


def dot_full(a, b, dims):
    return lax.dot_general(a, b, dims, precision=HIGHEST, preferred_element_type=F32)


def cuts_of(nh):
    cuts = []
    for h in range(2):
        start = 0
        while start < nh:
            width = min(4, nh - start) if nh - start != 5 else 5
            cuts.append((h, start, width))
            start += width
    return cuts


def kernel(
    nz, nt, factor,
    mom_hbm, grad_hbm, basis_hbm, high_hbm, low_hbm, ortho_out, scaled_high, scaled_low,
    mom, grad, bhi, blo, vbuf, part, proj, rsbuf,
    wbuf, ropp, rleft, rright, rodd, reven, aodd, aeven, across, wfin,
    gram, gslice, grs, gsum, gx, gall, elim,
    rhi, rlo, nbuf,
    load_sem, store_sem, v_send, v_z, v_l, v_r, v_o, v_a,
    w_send, w_z, w_l, w_r, w_o, w_a, r_send, r_odd, r_even, a_odd, a_even, r_l, r_r, r_o,
    s_send, s_recv,
):
    rows, cols = mom.shape
    nblk = cols // 128
    nh = nblk // 2
    half = nz // 2
    na = across.shape[1]
    nb = nh - na
    m = GROUPS // (nz * NX)
    f = lax.axis_index("fsdp")
    t = lax.axis_index("tensor")
    z, x = lax.div(f, NX), lax.rem(f, NX)
    left, right, opp = lax.rem(x + NX - 1, NX), lax.rem(x + 1, NX), lax.rem(x + 2, NX)

    def zmod(value):
        return lax.rem(value + nz, nz)

    def tmod(value):
        return lax.rem(value + nt, nt)

    def dev(zz, xx):
        return (zz * NX + xx, t)

    to_up, to_down = dev(zmod(z + 1), x), dev(zmod(z - 1), x)
    to_up2, to_down2 = dev(zmod(z + 2), x), dev(zmod(z - 2 + nz), x)
    to_left, to_right, to_opp = dev(z, left), dev(z, right), dev(z, opp)

    def remote(src, dst, send, recv, device):
        return pltpu.make_async_remote_copy(
            src_ref=src, dst_ref=dst, send_sem=send, recv_sem=recv,
            device_id=device, device_id_type=pl.DeviceIdType.MESH,
        )

    def wait(ref, sem):
        pltpu.make_async_copy(ref, ref, sem).wait()

    load_basis = pltpu.make_async_copy(basis_hbm, vbuf.at[pl.ds(f * m, m)], load_sem.at[0])
    load_mom = pltpu.make_async_copy(mom_hbm, mom, load_sem.at[1])
    load_grad = pltpu.make_async_copy(grad_hbm, grad, load_sem.at[2])
    load_basis.start()
    load_mom.start()
    load_grad.start()

    barrier = pltpu.get_barrier_semaphore()

    def greet(device):
        pl.semaphore_signal(barrier, inc=1, device_id=device, device_id_type=pl.DeviceIdType.MESH)

    def greet_t(r, carry):
        greet((f, tmod(t + r)))
        return carry

    lax.fori_loop(1, nt, greet_t, 0)
    near = [to_left, to_right, to_opp]
    near += [dev(zmod(z + r), x) for r in sorted({1 % nz, nz - 1, 2 % nz, nz - 2} - {0})]
    for device in near:
        greet(device)
    pl.semaphore_wait(barrier, (nt - 1) + len(near))

    def gather(buf, cut, send, sz, sl, sr, so, sa, early, hook):
        whole = buf.shape[1]

        def at(zz, xx):
            return buf.at[pl.ds((zz * NX + xx) * m, m), pl.ds(0, cut)]

        def late(zz, xx):
            return buf.at[pl.ds((zz * NX + xx) * m, m), pl.ds(cut, whole - cut)]

        def bundle(zz):
            return buf.at[pl.ds(zz * NX * m, NX * m), pl.ds(cut, whole - cut)]

        def onward(j, ref, sem):
            @pl.when(j + 2 <= half)
            def _():
                remote(ref, ref, send, sem, to_up2).start()

            @pl.when(j + 1 <= half)
            def _():
                remote(ref, ref, send, sem, to_up).start()

        def back(j, ref, sem):
            @pl.when(j + 2 < half)
            def _():
                remote(ref, ref, send, sem, to_down2).start()

            @pl.when(j + 1 < half)
            def _():
                remote(ref, ref, send, sem, to_down).start()

        def push(zz, xx, sem, device):
            remote(at(zz, xx), at(zz, xx), send, sem.at[zz], device).start()

        def spread(zz):
            push(zz, x, sl, to_right)
            push(zz, x, sr, to_left)

        def pass_right(zz):
            wait(at(zz, left), sl.at[zz])
            push(zz, left, so, to_right)

        def pass_left(zz):
            wait(at(zz, right), sr.at[zz])
            push(zz, right, so, to_left)

        def late_ones(j):
            below, above = zmod(z - j), zmod(z + j)
            even = lax.rem(j, 2) == 0

            @pl.when((j > 0) & (j <= half))
            def _():
                wait(bundle(below), sa.at[below])
                pl.when(even)(lambda: onward(j, bundle(below), sa.at[below]))

            @pl.when((j > 0) & (j < half))
            def _():
                wait(bundle(above), sa.at[above])
                pl.when(even)(lambda: back(j, bundle(above), sa.at[above]))

        def passing(j):
            @pl.when((j >= 0) & (j <= half))
            def _():
                pass_right(zmod(z - j))

            @pl.when((j > 0) & (j < half))
            def _():
                pass_left(zmod(z + j))

        for device in (to_right, to_left, to_opp):
            remote(late(z, x), late(z, x), send, sa.at[nz], device).start()
        onward(0, at(z, x), sz.at[z])
        back(0, at(z, x), sz.at[z])
        spread(z)
        early()
        wait(buf.at[pl.ds(0, (NX - 1) * m), pl.ds(cut, whole - cut)], sa.at[nz])
        onward(0, bundle(z), sa.at[z])
        back(0, bundle(z), sa.at[z])

        def step(j, carry):
            below, above = zmod(z - j), zmod(z + j)
            even = lax.rem(j, 2) == 0
            wait(at(below, x), sz.at[below])

            @pl.when(even)
            def _():
                onward(j, at(below, x), sz.at[below])

            @pl.when(j < half)
            def _():
                wait(at(above, x), sz.at[above])

                @pl.when(even)
                def _():
                    back(j, at(above, x), sz.at[above])

            spread(below)

            @pl.when(j < half)
            def _():
                spread(above)

            late_ones(j - LAG_A)
            passing(j - LAG)
            hook(j)
            return carry

        lax.fori_loop(1, half + 1, step, 0)
        rest = max(LAG, LAG_A)

        def drain(j, carry):
            late_ones(j - LAG_A)
            passing(j - LAG)
            return carry

        lax.fori_loop(half + 1, half + 1 + rest, drain, 0)

        def finish(j, carry):
            below, above = zmod(z - j), zmod(z + j)
            wait(at(below, right), sr.at[below])
            wait(at(below, opp), so.at[below])

            @pl.when((j > 0) & (j < half))
            def _():
                wait(at(above, left), sl.at[above])
                wait(at(above, opp), so.at[above])

            return carry

        lax.fori_loop(0, half + 1, finish, 0)
        wait(buf.at[pl.ds(0, (nz * NX - 1) * m)], send)

    load_basis.wait()

    def make_blend():
        load_mom.wait()
        load_grad.wait()

        def body(c, carry):
            cut = pl.ds(pl.multiple_of(c * 256, 256), 256)
            blend = mom[:, cut] + grad[:, cut].astype(F32)
            mom[:, cut] = blend
            bhi[:, cut], blo[:, cut] = split(blend)
            return carry

        lax.fori_loop(0, nblk // 2, body, 0)

    gather(vbuf, 2 * nb, v_send.at[0], v_z, v_l, v_r, v_o, v_a, make_blend, lambda j: None)

    def project(c, acc):
        cut = pl.ds(pl.multiple_of(c * 256, 256), 256)
        pair = [vbuf[:, 2 * c + k].reshape(RANK, 128) for k in range(2)]
        return acc + dot3((bhi[:, cut], blo[:, cut]), split(jnp.concatenate(pair, axis=1)), NT)

    part[...] = lax.fori_loop(0, nblk // 2, project, jnp.zeros((rows, RANK), F32), unroll=UNROLL)

    share = rows // nt
    if nt > 1:
        own = pl.ds(t * share, share)

        def send_part(r, carry):
            peer = tmod(t + r)
            remote(
                part.at[pl.ds(peer * share, share)], rsbuf.at[r - 1],
                s_send.at[0], s_recv.at[0], (f, peer),
            ).start()
            return carry

        lax.fori_loop(1, nt, send_part, 0)
        wait(rsbuf, s_recv.at[0])
        total = part[own]
        for r in range(nt - 1):
            total = total + rsbuf[r]
        proj[own] = total

        def send_sum(r, carry):
            remote(
                proj.at[own], proj.at[own], s_send.at[1], s_recv.at[1], (f, tmod(t + r))
            ).start()
            return carry

        lax.fori_loop(1, nt, send_sum, 0)
        wait(proj.at[pl.ds(0, (nt - 1) * share)], s_recv.at[1])
        wait(rsbuf, s_send.at[0])
        wait(proj.at[pl.ds(0, (nt - 1) * share)], s_send.at[1])
    else:
        proj[...] = part[...]

    full = proj[...]
    gram[...] = dot_full(full, full, TN)
    gshare = RANK // nt
    ng = 2 * gshare // 4
    mg = ng // nz
    mine = gram[pl.ds(t * gshare, gshare), :]
    for r in range(gshare // 4):
        for c in range(2):
            gslice[2 * r + c] = mine[4 * r : 4 * r + 4, 128 * c : 128 * c + 128]

    def gram_send():
        def body(r, carry):
            peer = zmod(z + r)
            remote(
                gslice.at[pl.ds(peer * mg, mg)], grs.at[r - 1],
                s_send.at[2], s_recv.at[2], dev(peer, x),
            ).start()
            return carry

        lax.fori_loop(1, nz, body, 0)

    def gram_over_z():
        wait(grs, s_recv.at[2])
        gsum[...] = gslice[pl.ds(z * mg, mg)] + jnp.sum(grs[...], axis=0)
        gx[x] = gsum[...]
        for k, device in enumerate((to_left, to_right, to_opp)):
            remote(gsum, gx.at[x], s_send.at[3], s_recv.at[3], device).start()

    def gram_over_x():
        wait(gx.at[pl.ds(0, NX - 1)], s_recv.at[3])
        here = pl.ds(t * ng + z * mg, mg)
        gall[here] = jnp.sum(gx[...], axis=0)

        def body(r, carry):
            remote(
                gall.at[here], gall.at[here], s_send.at[4], s_recv.at[4], dev(zmod(z + r), x)
            ).start()
            return carry

        lax.fori_loop(1, nz, body, 0)

    def gram_over_t():
        wait(gall.at[pl.ds(0, (nz - 1) * mg)], s_recv.at[4])
        if nt > 1:
            here = pl.ds(t * ng, ng)

            def body(r, carry):
                remote(
                    gall.at[here], gall.at[here], s_send.at[5], s_recv.at[5], (f, tmod(t + r))
                ).start()
                return carry

            lax.fori_loop(1, nt, body, 0)

    def gram_done():
        if nt > 1:
            wait(gall.at[pl.ds(0, (nt - 1) * ng)], s_recv.at[5])
            wait(gall.at[pl.ds(0, (nt - 1) * ng)], s_send.at[5])
        wait(grs, s_send.at[2])
        wait(gx.at[pl.ds(0, NX - 1)], s_send.at[3])
        wait(gall.at[pl.ds(0, (nz - 1) * mg)], s_send.at[4])
        for r in range(RANK // 8):
            for c in range(2):
                pair = [gall[4 * r + c], gall[4 * r + 2 + c]]
                elim[8 * r : 8 * r + 8, 128 * c : 128 * c + 128] = jnp.concatenate(pair, axis=0)
        down = lax.broadcasted_iota(jnp.int32, (RANK, RANK), 0)
        across = lax.broadcasted_iota(jnp.int32, (RANK, RANK), 1)
        elim[:, RANK:] = jnp.where(down == across, 1.0, 0.0).astype(F32)

    gram_send()

    turned = split(full.T)
    for h, start, width in cuts_of(nh):
        cut = slice((h * nh + start) * 128, (h * nh + start + width) * 128)
        out = dot3(turned, (bhi[:, cut], blo[:, cut]), NN)
        for k in range(width):
            for r in range(RANK // 8):
                wbuf[2 * r + h, start + k] = out[8 * r : 8 * r + 8, 128 * k : 128 * k + 128]

    def piece(buf, index):
        return buf.at[pl.ds(index * m, m)]

    def wat(q, xx):
        return wbuf.at[pl.ds((q * NX + xx) * m, m), pl.ds(0, nb)]

    def wlate(q, xx):
        return wbuf.at[pl.ds((q * NX + xx) * m, m), pl.ds(nb, na)]

    def wbundle(q):
        return wbuf.at[pl.ds(q * NX * m, NX * m), pl.ds(nb, na)]

    def slots(buf, index):
        return buf.at[pl.ds(index * NX * m, NX * m)]

    def add_into(ref, other):
        ref[...] = ref[...] + other[...]

    def stage_a(q, s):
        remote(wat(q, opp), piece(ropp, q), r_send.at[0], r_o.at[q], (to_right, to_left)[s]).start()

    def stage_b(q, s):
        wait(piece(ropp, q), r_o.at[q])
        add_into(wat(q, (right, left)[s]), piece(ropp, q))
        remote(wat(q, right), piece(rleft, q), r_send.at[0], r_l.at[q], to_right).start()
        remote(wat(q, left), piece(rright, q), r_send.at[0], r_r.at[q], to_left).start()

    def stage_c(q):
        wait(piece(rleft, q), r_l.at[q])
        wait(piece(rright, q), r_r.at[q])
        here = wat(q, x)
        here[...] = here[...] + (piece(rleft, q)[...] + piece(rright, q)[...])

    def z_sum(j, top, q, ref, place, odd, even, s_odd, s_even, to_one, to_two, up):
        def slot(last):
            return jnp.where(last, nz, q) if up else q

        is_odd = lax.rem(j, 2) == 1

        @pl.when(is_odd & (j <= top))
        def _():
            at = slot(j == 1)
            remote(ref, place(odd, at), r_send.at[0], s_odd.at[at], to_one).start()

        @pl.when(jnp.logical_not(is_odd) & (j >= 2) & (j <= top))
        def _():
            @pl.when(j + 1 <= top)
            def _():
                wait(place(odd, q), s_odd.at[q])
                add_into(ref, place(odd, q))

            @pl.when(j + 2 <= top)
            def _():
                wait(place(even, q), s_even.at[q])
                add_into(ref, place(even, q))

            at = slot(j == 2)
            remote(ref, place(even, at), r_send.at[0], s_even.at[at], to_two).start()

    def z_last(ref, place, odd, even, s_odd, s_even):
        for buf, sem, index, there in (
            (odd, s_odd, z, half >= 1), (even, s_even, z, half >= 2),
            (odd, s_odd, nz, half >= 2), (even, s_even, nz, half >= 3),
        ):
            if there:
                wait(place(buf, index), sem.at[index])
                add_into(ref, place(buf, index))

    def early_sum(j):
        args = (slots, aodd, aeven, a_odd, a_even)
        q = zmod(z - j)
        z_sum(j, half, q, wbundle(q), *args, to_down, to_down2, False)
        q = zmod(z + j)
        z_sum(j, half - 1, q, wbundle(q), *args, to_up, to_up2, True)

        @pl.when(j == 0)
        def _():
            z_last(wbundle(z), *args)
            for xx, device in ((left, to_left), (right, to_right), (opp, to_opp)):
                remote(wlate(z, xx), piece(across, x), r_send.at[0], a_odd.at[nz + 1], device).start()
            piece(across, x)[...] = wlate(z, x)[...]

    def late_sum(j):
        args = (piece, rodd, reven, r_odd, r_even)
        q = zmod(z - j)
        stage_c(q)
        z_sum(j, half, q, wat(q, x), *args, to_down, to_down2, False)

        @pl.when((j >= 1) & (j < half))
        def _():
            q = zmod(z + j)
            stage_c(q)
            z_sum(j, half - 1, q, wat(q, x), *args, to_up, to_up2, True)

        @pl.when(j == 0)
        def _():
            z_last(wat(z, x), *args)

    lane = lax.broadcasted_iota(jnp.int32, (PANEL, 128), 1)
    down = lax.broadcasted_iota(jnp.int32, (PANEL, 128), 0)
    wide = lax.broadcasted_iota(jnp.int32, (PANEL, RANK), 1)
    npanel = RANK // PANEL

    def panel(b):
        here = pl.ds(pl.multiple_of(b * PANEL, PANEL), PANEL)
        block = elim[here, :]
        turned = pltpu.roll(block[:, :RANK], lax.rem(RANK - b * PANEL, RANK), 1)[:, :128]
        state = jnp.where(lane < PANEL, turned, jnp.where(lane == down + PANEL, 1.0, 0.0))
        for first in range(0, PANEL, MINI):
            spread = [
                jnp.broadcast_to(state[:, k : k + 1], (PANEL, 128)) for k in range(first, first + MINI)
            ]
            for k in range(min(MINI, PANEL - 1 - first)):
                j = first + k
                scale = jnp.where(down > j, spread[k], 0.0) * (1.0 / spread[k][j : j + 1, :])
                state = state - scale * state[j : j + 1, :]
                for n in range(k + 1, MINI):
                    spread[n] = spread[n] - scale * spread[n][j : j + 1, :]
        diag = jnp.sum(jnp.where(lane == down, state, 0.0), axis=1, keepdims=True)
        lower = state[:, PANEL : 2 * PANEL] / jnp.sqrt(diag)
        done = dot_full(lower, block, NN)
        rest = jnp.where(wide >= (b + 1) * PANEL, done[:, :RANK], 0.0)
        (rh, rm, rl), (dh, dm, dl) = split3(rest), split3(done)
        elim[...] = elim[...] - dot(
            jnp.concatenate([rh, rh, rh, rm, rm, rl], axis=0),
            jnp.concatenate([dh, dm, dl, dh, dm, dh], axis=0),
            TN,
        )
        elim[here, :] = done

    def reduce_step(i, carry):
        @pl.when(i <= half)
        def _():
            stage_a(zmod(z - half + i), 0)

        @pl.when((i >= 1) & (i < half))
        def _():
            stage_a(zmod(z + half - i), 1)

        b = i - LAG_B

        @pl.when((b >= 0) & (b <= half))
        def _():
            stage_b(zmod(z - half + b), 0)

        @pl.when((b >= 1) & (b < half))
        def _():
            stage_b(zmod(z + half - b), 1)

        @pl.when((i >= LAG_S) & (i <= half + LAG_S))
        def _():
            early_sum(half + LAG_S - i)

        @pl.when(i >= LAG_C)
        def _():
            late_sum(half + LAG_C - i)

        last = half + LAG_C
        for place, work in zip(GRAM_AT, (gram_over_z, gram_over_x, gram_over_t, gram_done)):
            pl.when(i == min(place, last))(work)

        @pl.when(i > max(GRAM_AT))
        def _():
            panel(i - max(GRAM_AT) - 1)

        return carry

    lax.fori_loop(0, half + 1 + LAG_C, reduce_step, 0)
    wait(across.at[pl.ds(0, (NX - 1) * m)], a_odd.at[nz + 1])
    wfin[pl.ds(f * m, m), 0:nb] = wat(z, x)[...]
    wfin[pl.ds(f * m, m), nb:] = jnp.sum(across[...].reshape(NX, m, na, 8, 128), axis=0)

    begun = max(0, half + LAG_C - max(GRAM_AT))

    def panels(j):
        per = -(-(npanel - begun) // max(half // 2, 1))

        @pl.when(lax.rem(j, 2) == (0 if half > 1 else 1))
        def _():
            for k in range(per):
                b = begun + (lax.div(j, 2) - (1 if half > 1 else 0)) * per + k
                pl.when(b < npanel)(functools.partial(panel, b))

    gather(wfin, nb, w_send.at[0], w_z, w_l, w_r, w_o, w_a, lambda: None, panels)
    wait(wbuf.at[pl.ds(0, (nz * NX - 1) * m)], r_send.at[0])

    inv_lower = elim[:, RANK:]
    ortho = dot_full(proj[...], inv_lower, NT)
    low = split(inv_lower)
    squared = jnp.zeros((RANK, 128), F32)
    stores = []
    for n, (h, start, width) in enumerate(cuts_of(nh)):
        cut = slice((h * nh + start) * 128, (h * nh + start + width) * 128)
        columns = [
            jnp.concatenate([wfin[2 * r + h, start + k] for r in range(RANK // 8)], axis=0)
            for k in range(width)
        ]
        out = dot3(low, split(jnp.concatenate(columns, axis=1)), NN)
        for k in range(width):
            one = out[:, 128 * k : 128 * k + 128]
            squared = squared + one * one
        rhi[:, cut], rlo[:, cut] = split(out)
        for k, (buf, hbm) in enumerate(((rhi, high_hbm), (rlo, low_hbm))):
            stores.append(pltpu.make_async_copy(buf.at[:, cut], hbm.at[:, cut], store_sem.at[2 * n + k]))
            stores[-1].start()
    nbuf[t] = dot_full(jnp.ones((8, 128), F32), squared, NT)

    if nt > 1:
        def send_norm(r, carry):
            remote(
                nbuf.at[t], nbuf.at[t], s_send.at[6], s_recv.at[6], (f, tmod(t + r))
            ).start()
            return carry

        lax.fori_loop(1, nt, send_norm, 0)

    ortho_out[...] = ortho.astype(BF16)
    if nt > 1:
        wait(nbuf.at[pl.ds(0, nt - 1)], s_recv.at[6])
        wait(nbuf.at[pl.ds(0, nt - 1)], s_send.at[6])
    norm = nbuf[0]
    for r in range(1, nt):
        norm = norm + nbuf[r]
    inverse = 1.0 / (jnp.sqrt(norm) + 1e-06)
    scaled_high[...], scaled_low[...] = split(ortho * (inverse[0:1, :] * -factor))
    for store in stores:
        store.wait()


def update(
    mom_hbm, grad_hbm, high_hbm, low_hbm, ortho, scaled_high, scaled_low, newm_hbm, delta_hbm,
    mom, grad, rhi, rlo, dout, load_sem, store_sem,
):
    cuts = cuts_of(mom.shape[1] // 256)
    nh = mom.shape[1] // 256
    pairs = ((high_hbm, rhi), (low_hbm, rlo), (mom_hbm, mom), (grad_hbm, grad))
    loads, stores = [], []
    for n, (h, start, width) in enumerate(cuts):
        cut = slice((h * nh + start) * 128, (h * nh + start + width) * 128)
        for k, (hbm, buf) in enumerate(pairs):
            loads.append(pltpu.make_async_copy(hbm.at[:, cut], buf.at[:, cut], load_sem.at[4 * n + k]))
            loads[-1].start()
    both = jnp.concatenate([scaled_high[...], scaled_low[...], ortho[...]], axis=0)
    rows = ortho.shape[0]
    for n, (h, start, width) in enumerate(cuts):
        cut = slice((h * nh + start) * 128, (h * nh + start + width) * 128)
        for load in loads[4 * n : 4 * n + 4]:
            load.wait()
        high = dot(both, rhi[:, cut], NN)
        delta = high[:rows] + (high[rows : 2 * rows] + dot(scaled_high[...], rlo[:, cut], NN))
        dout[:, cut] = delta.astype(BF16)
        mom[:, cut] = (mom[:, cut] + grad[:, cut].astype(F32)) - 0.05 * high[2 * rows :]
        for k, (buf, hbm) in enumerate(((mom, newm_hbm), (dout, delta_hbm))):
            stores.append(pltpu.make_async_copy(buf.at[:, cut], hbm.at[:, cut], store_sem.at[2 * n + k]))
            stores[-1].start()
    for store in stores:
        store.wait()


def per_device(nz, nt, factor, momentum, gradient, basis):
    rows, cols = momentum.shape
    nblk = cols // 128
    nh = nblk // 2
    m = GROUPS // (nz * NX)
    gshare = RANK // nt
    ng = 2 * gshare // 4
    mg = ng // nz
    na = min(NA, nh - 1)
    nb = nh - na
    tiles = basis.reshape(m, 4, nblk, 128).transpose(0, 2, 1, 3)
    vmem = pltpu.VMEM
    dma = pltpu.SemaphoreType.DMA
    any_spec = pl.BlockSpec(memory_space=pl.ANY)
    one = max(nt - 1, 1)
    vmem_spec = pl.BlockSpec(memory_space=pltpu.VMEM)
    ncut = len(cuts_of(nh))
    high, low, ortho, scaled_high, scaled_low = pl.pallas_call(
        functools.partial(kernel, nz, nt, factor),
        out_shape=(
            jax.ShapeDtypeStruct((RANK, cols), BF16),
            jax.ShapeDtypeStruct((RANK, cols), BF16),
            jax.ShapeDtypeStruct((rows, RANK), BF16),
            jax.ShapeDtypeStruct((rows, RANK), BF16),
            jax.ShapeDtypeStruct((rows, RANK), BF16),
        ),
        in_specs=[any_spec] * 3,
        out_specs=(any_spec, any_spec, vmem_spec, vmem_spec, vmem_spec),
        scratch_shapes=[
            vmem((rows, cols), F32),
            vmem((rows, cols), BF16),
            vmem((rows, cols), BF16),
            vmem((rows, cols), BF16),
            vmem((GROUPS, nblk, 4, 128), F32),
            vmem((rows, RANK), F32),
            vmem((rows, RANK), F32),
            vmem((one, rows // nt, RANK), F32),
            vmem((GROUPS, nh, 8, 128), F32),
            vmem((nz * m, nb, 8, 128), F32),
            vmem((nz * m, nb, 8, 128), F32),
            vmem((nz * m, nb, 8, 128), F32),
            vmem(((nz + 1) * m, nb, 8, 128), F32),
            vmem(((nz + 1) * m, nb, 8, 128), F32),
            vmem(((nz + 1) * NX * m, na, 8, 128), F32),
            vmem(((nz + 1) * NX * m, na, 8, 128), F32),
            vmem((NX * m, na, 8, 128), F32),
            vmem((GROUPS, nh, 8, 128), F32),
            vmem((RANK, RANK), F32),
            vmem((ng, 4, 128), F32),
            vmem((nz - 1, mg, 4, 128), F32),
            vmem((mg, 4, 128), F32),
            vmem((NX, mg, 4, 128), F32),
            vmem((2 * GROUPS, 4, 128), F32),
            vmem((RANK, 2 * RANK), F32),
            vmem((RANK, cols), BF16),
            vmem((RANK, cols), BF16),
            vmem((nt, 8, RANK), F32),
            dma((3,)),
            dma((2 * ncut,)),
            dma((1,)), dma((nz,)), dma((nz,)), dma((nz,)), dma((nz,)), dma((nz + 1,)),
            dma((1,)), dma((nz,)), dma((nz,)), dma((nz,)), dma((nz,)), dma((nz + 1,)),
            dma((1,)), dma((nz + 1,)), dma((nz + 1,)), dma((nz + 2,)), dma((nz + 1,)),
            dma((nz,)), dma((nz,)), dma((nz,)),
            dma((7,)),
            dma((7,)),
        ],
        compiler_params=pltpu.CompilerParams(
            collective_id=0, has_side_effects=True, vmem_limit_bytes=56 * 2**20
        ),
        name="dion_step",
    )(momentum, gradient, tiles)
    return pl.pallas_call(
        update,
        out_shape=(
            jax.ShapeDtypeStruct((rows, cols), F32),
            jax.ShapeDtypeStruct((rows, cols), BF16),
        ),
        in_specs=[any_spec] * 4 + [vmem_spec] * 3,
        out_specs=(any_spec, any_spec),
        scratch_shapes=[
            vmem((rows, cols), F32),
            vmem((rows, cols), BF16),
            vmem((RANK, cols), BF16),
            vmem((RANK, cols), BF16),
            vmem((rows, cols), BF16),
            dma((4 * ncut,)),
            dma((2 * ncut,)),
        ],
        compiler_params=pltpu.CompilerParams(vmem_limit_bytes=56 * 2**20),
        name="dion_update",
    )(momentum, gradient, high, low, ortho, scaled_high, scaled_low)


def solution(mesh):
    nz, nt = mesh.shape["fsdp"] // NX, mesh.shape["tensor"]
    factor = (ROWS * COLS / RANK) ** 0.5
    spec = P("fsdp", "tensor")
    return jax.shard_map(
        functools.partial(per_device, nz, nt, factor),
        mesh=mesh, in_specs=(spec,) * 3, out_specs=(spec,) * 2, check_vma=False,
    )
```

```python
import functools

import jax
import jax.numpy as jnp
from jax import lax
from jax.experimental import pallas as pl
from jax.experimental.pallas import tpu as pltpu
from jax.sharding import PartitionSpec as P

ROWS = 8192
COLS = 26624
RANK = 256
NX = 4
GROUPS = RANK // 4
PANEL = 32
MINI = 16
NA = 2
LAG = 2
LAG_A = 2
UNROLL = 13
LAG_S = 1
LAG_B = 1
LAG_C = 3
GRAM_AT = (2, 4, 6, 9)
F32 = jnp.float32
BF16 = jnp.bfloat16
HIGHEST = lax.Precision.HIGHEST
NT = (((1,), (1,)), ((), ()))
TN = (((0,), (0,)), ((), ()))
NN = (((1,), (0,)), ((), ()))


def split3(value):
    high = value.astype(BF16)
    rest = value - high.astype(F32)
    mid = rest.astype(BF16)
    return high, mid, (rest - mid.astype(F32)).astype(BF16)


def split(value):
    high = value.astype(BF16)
    return high, (value - high.astype(F32)).astype(BF16)


def dot(a, b, dims):
    return lax.dot_general(a, b, dims, preferred_element_type=F32)


def dot3(a, b, dims):
    (ah, al), (bh, bl) = a, b
    return dot(ah, bh, dims) + (dot(ah, bl, dims) + dot(al, bh, dims))


def dot_full(a, b, dims):
    return lax.dot_general(a, b, dims, precision=HIGHEST, preferred_element_type=F32)


def cuts_of(nh):
    cuts = []
    for h in range(2):
        start = 0
        while start < nh:
            width = min(4, nh - start) if nh - start != 5 else 5
            cuts.append((h, start, width))
            start += width
    return cuts


def kernel(
    nz, nt, factor,
    mom_hbm, grad_hbm, basis_hbm, high_hbm, low_hbm, ortho_out, scaled_high, scaled_low,
    mom, grad, bhi, blo, vbuf, part, proj, rsbuf,
    wbuf, ropp, rleft, rright, rodd, reven, aodd, aeven, across, wfin,
    gram, gslice, grs, gsum, gx, gall, elim,
    rhi, rlo, nbuf, ortho_f32, lhi, llo,
    load_sem, store_sem, v_send, v_z, v_l, v_r, v_o, v_a,
    w_send, w_z, w_l, w_r, w_o, w_a, r_send, r_odd, r_even, a_odd, a_even, r_l, r_r, r_o,
    s_send, s_recv,
):
    rows, cols = mom.shape
    nblk = cols // 128
    nh = nblk // 2
    half = nz // 2
    na = across.shape[1]
    nb = nh - na
    m = GROUPS // (nz * NX)
    f = lax.axis_index("fsdp")
    t = lax.axis_index("tensor")
    z, x = lax.div(f, NX), lax.rem(f, NX)
    left, right, opp = lax.rem(x + NX - 1, NX), lax.rem(x + 1, NX), lax.rem(x + 2, NX)

    def zmod(value):
        return lax.rem(value + nz, nz)

    def tmod(value):
        return lax.rem(value + nt, nt)

    def dev(zz, xx):
        return (zz * NX + xx, t)

    to_up, to_down = dev(zmod(z + 1), x), dev(zmod(z - 1), x)
    to_up2, to_down2 = dev(zmod(z + 2), x), dev(zmod(z - 2 + nz), x)
    to_left, to_right, to_opp = dev(z, left), dev(z, right), dev(z, opp)

    def remote(src, dst, send, recv, device):
        return pltpu.make_async_remote_copy(
            src_ref=src, dst_ref=dst, send_sem=send, recv_sem=recv,
            device_id=device, device_id_type=pl.DeviceIdType.MESH,
        )

    def wait(ref, sem):
        pltpu.make_async_copy(ref, ref, sem).wait()

    load_basis = pltpu.make_async_copy(basis_hbm, vbuf.at[pl.ds(f * m, m)], load_sem.at[0])
    load_mom = pltpu.make_async_copy(mom_hbm, mom, load_sem.at[1])
    load_grad = pltpu.make_async_copy(grad_hbm, grad, load_sem.at[2])
    load_basis.start()
    load_mom.start()
    load_grad.start()

    barrier = pltpu.get_barrier_semaphore()

    def greet(device):
        pl.semaphore_signal(barrier, inc=1, device_id=device, device_id_type=pl.DeviceIdType.MESH)

    def greet_t(r, carry):
        greet((f, tmod(t + r)))
        return carry

    lax.fori_loop(1, nt, greet_t, 0)
    near = [to_left, to_right, to_opp]
    near += [dev(zmod(z + r), x) for r in sorted({1 % nz, nz - 1, 2 % nz, nz - 2} - {0})]
    for device in near:
        greet(device)
    pl.semaphore_wait(barrier, (nt - 1) + len(near))

    def gather(buf, cut, send, sz, sl, sr, so, sa, early, hook, tail):
        whole = buf.shape[1]

        def at(zz, xx):
            return buf.at[pl.ds((zz * NX + xx) * m, m), pl.ds(0, cut)]

        def late(zz, xx):
            return buf.at[pl.ds((zz * NX + xx) * m, m), pl.ds(cut, whole - cut)]

        def bundle(zz):
            return buf.at[pl.ds(zz * NX * m, NX * m), pl.ds(cut, whole - cut)]

        def onward(j, ref, sem):
            @pl.when(j + 2 <= half)
            def _():
                remote(ref, ref, send, sem, to_up2).start()

            @pl.when(j + 1 <= half)
            def _():
                remote(ref, ref, send, sem, to_up).start()

        def back(j, ref, sem):
            @pl.when(j + 2 < half)
            def _():
                remote(ref, ref, send, sem, to_down2).start()

            @pl.when(j + 1 < half)
            def _():
                remote(ref, ref, send, sem, to_down).start()

        def push(zz, xx, sem, device):
            remote(at(zz, xx), at(zz, xx), send, sem.at[zz], device).start()

        def spread(zz):
            push(zz, x, sl, to_right)
            push(zz, x, sr, to_left)

        def pass_right(zz):
            wait(at(zz, left), sl.at[zz])
            push(zz, left, so, to_right)

        def pass_left(zz):
            wait(at(zz, right), sr.at[zz])
            push(zz, right, so, to_left)

        def late_ones(j):
            below, above = zmod(z - j), zmod(z + j)
            even = lax.rem(j, 2) == 0

            @pl.when((j > 0) & (j <= half))
            def _():
                wait(bundle(below), sa.at[below])
                pl.when(even)(lambda: onward(j, bundle(below), sa.at[below]))

            @pl.when((j > 0) & (j < half))
            def _():
                wait(bundle(above), sa.at[above])
                pl.when(even)(lambda: back(j, bundle(above), sa.at[above]))

        def passing(j):
            @pl.when(j == 0)
            def _():
                pass_left(z)

            @pl.when((j > 0) & (j < half))
            def _():
                pass_right(zmod(z - j))
                pass_left(zmod(z + j))

        for device in (to_right, to_left, to_opp):
            remote(late(z, x), late(z, x), send, sa.at[nz], device).start()
        onward(0, at(z, x), sz.at[z])
        back(0, at(z, x), sz.at[z])
        spread(z)
        early()
        wait(buf.at[pl.ds(0, (NX - 1) * m), pl.ds(cut, whole - cut)], sa.at[nz])
        onward(0, bundle(z), sa.at[z])
        back(0, bundle(z), sa.at[z])

        def step(j, carry):
            below, above = zmod(z - j), zmod(z + j)
            even = lax.rem(j, 2) == 0
            wait(at(below, x), sz.at[below])

            @pl.when(even)
            def _():
                onward(j, at(below, x), sz.at[below])

            @pl.when(j < half)
            def _():
                wait(at(above, x), sz.at[above])

                @pl.when(even)
                def _():
                    back(j, at(above, x), sz.at[above])

            spread(below)

            @pl.when(j < half)
            def _():
                spread(above)

            pl.when(j == half)(lambda: push(below, x, so, to_opp))
            late_ones(j - LAG_A)
            passing(j - LAG)
            hook(j)
            return carry

        lax.fori_loop(1, half + 1, step, 0)
        rest = max(LAG, LAG_A)

        def drain(j, carry):
            late_ones(j - LAG_A)
            passing(j - LAG)
            return carry

        lax.fori_loop(half + 1, half + 1 + rest, drain, 0)

        def finish(j, carry):
            below, above = zmod(z - j), zmod(z + j)
            wait(at(below, opp), so.at[below])
            pl.when(j > 0)(lambda: wait(at(below, right), sr.at[below]))
            pl.when((j == 0) | (j == half))(lambda: wait(at(below, left), sl.at[below]))

            @pl.when((j > 0) & (j < half))
            def _():
                wait(at(above, left), sl.at[above])
                wait(at(above, opp), so.at[above])

            return carry

        tail()
        lax.fori_loop(0, half + 1, finish, 0)

    load_basis.wait()

    def make_blend():
        load_mom.wait()
        load_grad.wait()

        def body(c, carry):
            cut = pl.ds(pl.multiple_of(c * 256, 256), 256)
            blend = mom[:, cut] + grad[:, cut].astype(F32)
            mom[:, cut] = blend
            bhi[:, cut], blo[:, cut] = split(blend)
            return carry

        lax.fori_loop(0, nblk // 2, body, 0)

    gather(vbuf, 2 * nb, v_send.at[0], v_z, v_l, v_r, v_o, v_a, make_blend, lambda j: None, lambda: None)

    def project(c, acc):
        cut = pl.ds(pl.multiple_of(c * 256, 256), 256)
        pair = [vbuf[:, 2 * c + k].reshape(RANK, 128) for k in range(2)]
        return acc + dot3((bhi[:, cut], blo[:, cut]), split(jnp.concatenate(pair, axis=1)), NT)

    part[...] = lax.fori_loop(0, nblk // 2, project, jnp.zeros((rows, RANK), F32), unroll=UNROLL)

    share = rows // nt
    if nt > 1:
        own = pl.ds(t * share, share)

        def send_part(r, carry):
            peer = tmod(t + r)
            remote(
                part.at[pl.ds(peer * share, share)], rsbuf.at[r - 1],
                s_send.at[0], s_recv.at[0], (f, peer),
            ).start()
            return carry

        lax.fori_loop(1, nt, send_part, 0)
        wait(rsbuf, s_recv.at[0])
        total = part[own]
        for r in range(nt - 1):
            total = total + rsbuf[r]
        proj[own] = total

        def send_sum(r, carry):
            remote(
                proj.at[own], proj.at[own], s_send.at[1], s_recv.at[1], (f, tmod(t + r))
            ).start()
            return carry

        lax.fori_loop(1, nt, send_sum, 0)
        wait(proj.at[pl.ds(0, (nt - 1) * share)], s_recv.at[1])
    else:
        proj[...] = part[...]

    full = proj[...]
    gshare = RANK // nt
    ng = 2 * gshare // 4
    mg = ng // nz

    def make_gram():
        square = proj[...]
        gram[...] = dot_full(square, square, TN)
        mine = gram[pl.ds(t * gshare, gshare), :]
        for r in range(gshare // 4):
            for c in range(2):
                gslice[2 * r + c] = mine[4 * r : 4 * r + 4, 128 * c : 128 * c + 128]

    def gram_send():
        make_gram()

        def body(r, carry):
            peer = zmod(z + r)
            remote(
                gslice.at[pl.ds(peer * mg, mg)], grs.at[r - 1],
                s_send.at[2], s_recv.at[2], dev(peer, x),
            ).start()
            return carry

        lax.fori_loop(1, nz, body, 0)

    def gram_over_z():
        wait(grs, s_recv.at[2])
        gsum[...] = gslice[pl.ds(z * mg, mg)] + jnp.sum(grs[...], axis=0)
        gx[x] = gsum[...]
        for k, device in enumerate((to_left, to_right, to_opp)):
            remote(gsum, gx.at[x], s_send.at[3], s_recv.at[3], device).start()

    def gram_over_x():
        wait(gx.at[pl.ds(0, NX - 1)], s_recv.at[3])
        here = pl.ds(t * ng + z * mg, mg)
        gall[here] = jnp.sum(gx[...], axis=0)

        def body(r, carry):
            remote(
                gall.at[here], gall.at[here], s_send.at[4], s_recv.at[4], dev(zmod(z + r), x)
            ).start()
            return carry

        lax.fori_loop(1, nz, body, 0)

    def gram_over_t():
        wait(gall.at[pl.ds(0, (nz - 1) * mg)], s_recv.at[4])
        if nt > 1:
            here = pl.ds(t * ng, ng)

            def body(r, carry):
                remote(
                    gall.at[here], gall.at[here], s_send.at[5], s_recv.at[5], (f, tmod(t + r))
                ).start()
                return carry

            lax.fori_loop(1, nt, body, 0)

    def gram_done():
        if nt > 1:
            wait(gall.at[pl.ds(0, (nt - 1) * ng)], s_recv.at[5])
        for r in range(RANK // 8):
            for c in range(2):
                pair = [gall[4 * r + c], gall[4 * r + 2 + c]]
                elim[8 * r : 8 * r + 8, 128 * c : 128 * c + 128] = jnp.concatenate(pair, axis=0)
        down = lax.broadcasted_iota(jnp.int32, (RANK, RANK), 0)
        across = lax.broadcasted_iota(jnp.int32, (RANK, RANK), 1)
        elim[:, RANK:] = jnp.where(down == across, 1.0, 0.0).astype(F32)

    turned = split(full.T)
    for h, start, width in cuts_of(nh):
        cut = slice((h * nh + start) * 128, (h * nh + start + width) * 128)
        out = dot3(turned, (bhi[:, cut], blo[:, cut]), NN)
        for k in range(width):
            for r in range(RANK // 8):
                wbuf[2 * r + h, start + k] = out[8 * r : 8 * r + 8, 128 * k : 128 * k + 128]

    def piece(buf, index):
        return buf.at[pl.ds(index * m, m)]

    def wat(q, xx):
        return wbuf.at[pl.ds((q * NX + xx) * m, m), pl.ds(0, nb)]

    def wlate(q, xx):
        return wbuf.at[pl.ds((q * NX + xx) * m, m), pl.ds(nb, na)]

    def wbundle(q):
        return wbuf.at[pl.ds(q * NX * m, NX * m), pl.ds(nb, na)]

    def slots(buf, index):
        return buf.at[pl.ds(index * NX * m, NX * m)]

    def add_into(ref, other):
        ref[...] = ref[...] + other[...]

    def stage_a(q, s):
        remote(wat(q, opp), piece(ropp, q), r_send.at[0], r_o.at[q], (to_right, to_left, to_opp)[s]).start()

    def stage_b(q, s):
        if s < 2:
            wait(piece(ropp, q), r_o.at[q])
            add_into(wat(q, (right, left)[s]), piece(ropp, q))
        remote(wat(q, right), piece(rleft, q), r_send.at[0], r_l.at[q], to_right).start()
        remote(wat(q, left), piece(rright, q), r_send.at[0], r_r.at[q], to_left).start()

    def stage_c(q):
        wait(piece(rleft, q), r_l.at[q])
        wait(piece(rright, q), r_r.at[q])
        here = wat(q, x)
        here[...] = here[...] + (piece(rleft, q)[...] + piece(rright, q)[...])

    def z_sum(j, top, q, ref, place, odd, even, s_odd, s_even, to_one, to_two, up):
        def slot(last):
            return jnp.where(last, nz, q) if up else q

        is_odd = lax.rem(j, 2) == 1

        @pl.when(is_odd & (j <= top))
        def _():
            at = slot(j == 1)
            remote(ref, place(odd, at), r_send.at[0], s_odd.at[at], to_one).start()

        @pl.when(jnp.logical_not(is_odd) & (j >= 2) & (j <= top))
        def _():
            @pl.when(j + 1 <= top)
            def _():
                wait(place(odd, q), s_odd.at[q])
                add_into(ref, place(odd, q))

            @pl.when(j + 2 <= top)
            def _():
                wait(place(even, q), s_even.at[q])
                add_into(ref, place(even, q))

            at = slot(j == 2)
            remote(ref, place(even, at), r_send.at[0], s_even.at[at], to_two).start()

    def z_last(ref, place, odd, even, s_odd, s_even):
        for buf, sem, index, there in (
            (odd, s_odd, z, half >= 1), (even, s_even, z, half >= 2),
            (odd, s_odd, nz, half >= 2), (even, s_even, nz, half >= 3),
        ):
            if there:
                wait(place(buf, index), sem.at[index])
                add_into(ref, place(buf, index))

    def early_sum(j):
        args = (slots, aodd, aeven, a_odd, a_even)
        q = zmod(z - j)
        z_sum(j, half, q, wbundle(q), *args, to_down, to_down2, False)
        q = zmod(z + j)
        z_sum(j, half - 1, q, wbundle(q), *args, to_up, to_up2, True)

        @pl.when(j == 0)
        def _():
            z_last(wbundle(z), *args)
            for xx, device in ((left, to_left), (right, to_right), (opp, to_opp)):
                remote(wlate(z, xx), piece(across, x), r_send.at[0], a_odd.at[nz + 1], device).start()
            piece(across, x)[...] = wlate(z, x)[...]

    def late_sum(j):
        args = (piece, rodd, reven, r_odd, r_even)
        q = zmod(z - j)
        stage_c(q)

        @pl.when(j == half)
        def _():
            wait(piece(ropp, q), r_o.at[q])
            add_into(wat(q, x), piece(ropp, q))

        z_sum(j, half, q, wat(q, x), *args, to_down, to_down2, False)

        @pl.when((j >= 1) & (j < half))
        def _():
            q = zmod(z + j)
            stage_c(q)
            z_sum(j, half - 1, q, wat(q, x), *args, to_up, to_up2, True)

        @pl.when(j == 0)
        def _():
            z_last(wat(z, x), *args)

    lane = lax.broadcasted_iota(jnp.int32, (PANEL, 128), 1)
    down = lax.broadcasted_iota(jnp.int32, (PANEL, 128), 0)
    wide = lax.broadcasted_iota(jnp.int32, (PANEL, RANK), 1)
    npanel = RANK // PANEL

    def panel(b):
        here = pl.ds(pl.multiple_of(b * PANEL, PANEL), PANEL)
        block = elim[here, :]
        turned = pltpu.roll(block[:, :RANK], lax.rem(RANK - b * PANEL, RANK), 1)[:, :128]
        state = jnp.where(lane < PANEL, turned, jnp.where(lane == down + PANEL, 1.0, 0.0))
        for first in range(0, PANEL, MINI):
            spread = [
                jnp.broadcast_to(state[:, k : k + 1], (PANEL, 128)) for k in range(first, first + MINI)
            ]
            for k in range(min(MINI, PANEL - 1 - first)):
                j = first + k
                scale = jnp.where(down > j, spread[k], 0.0) * (1.0 / spread[k][j : j + 1, :])
                state = state - scale * state[j : j + 1, :]
                for n in range(k + 1, MINI):
                    spread[n] = spread[n] - scale * spread[n][j : j + 1, :]
        diag = jnp.sum(jnp.where(lane == down, state, 0.0), axis=1, keepdims=True)
        lower = state[:, PANEL : 2 * PANEL] / jnp.sqrt(diag)
        done = dot_full(lower, block, NN)
        rest = jnp.where(wide >= (b + 1) * PANEL, done[:, :RANK], 0.0)
        (rh, rm, rl), (dh, dm, dl) = split3(rest), split3(done)
        elim[...] = elim[...] - dot(
            jnp.concatenate([rh, rh, rh, rm, rm, rl], axis=0),
            jnp.concatenate([dh, dm, dl, dh, dm, dh], axis=0),
            TN,
        )
        elim[here, :] = done

    def reduce_step(i, carry):
        @pl.when(i == 0)
        def _():
            q = zmod(z - half)
            stage_a(q, 2)
            stage_b(q, 2)

        @pl.when((i >= 1) & (i < half))
        def _():
            stage_a(zmod(z - half + i), 0)

        @pl.when((i >= 1) & (i <= half))
        def _():
            stage_a(zmod(z + half - i), 1)

        @pl.when(i >= LAG_C)
        def _():
            late_sum(half + LAG_C - i)

        @pl.when((i >= LAG_S) & (i <= half + LAG_S))
        def _():
            early_sum(half + LAG_S - i)

        b = i - LAG_B

        @pl.when((b >= 1) & (b < half))
        def _():
            stage_b(zmod(z - half + b), 0)

        @pl.when((b >= 1) & (b <= half))
        def _():
            stage_b(zmod(z + half - b), 1)

        pl.when(i == 0)(gram_send)
        last = half + LAG_C
        for place, work in zip(GRAM_AT, (gram_over_z, gram_over_x, gram_over_t, gram_done)):
            pl.when(i == min(place, last))(work)

        @pl.when(i > max(GRAM_AT))
        def _():
            panel(i - max(GRAM_AT) - 1)

        return carry

    lax.fori_loop(0, half + 1 + LAG_C, reduce_step, 0)
    wait(across.at[pl.ds(0, (NX - 1) * m)], a_odd.at[nz + 1])
    wfin[pl.ds(f * m, m), 0:nb] = wat(z, x)[...]
    wfin[pl.ds(f * m, m), nb:] = jnp.sum(across[...].reshape(NX, m, na, 8, 128), axis=0)

    def make_ortho():
        inv_lower = elim[:, RANK:]
        ortho_f32[...] = dot_full(proj[...], inv_lower, NT)
        lhi[...], llo[...] = split(inv_lower)

    begun = max(0, half + LAG_C - max(GRAM_AT))

    def panels(j):
        per = -(-(npanel - begun) // max(half // 2, 1))

        @pl.when(lax.rem(j, 2) == (0 if half > 1 else 1))
        def _():
            for k in range(per):
                b = begun + (lax.div(j, 2) - (1 if half > 1 else 0)) * per + k
                pl.when(b < npanel)(functools.partial(panel, b))

    gather(wfin, nb, w_send.at[0], w_z, w_l, w_r, w_o, w_a, lambda: None, panels, make_ortho)

    low = lhi[...], llo[...]
    squared = jnp.zeros((RANK, 128), F32)
    stores = []
    for n, (h, start, width) in enumerate(cuts_of(nh)):
        cut = slice((h * nh + start) * 128, (h * nh + start + width) * 128)
        columns = [
            jnp.concatenate([wfin[2 * r + h, start + k] for r in range(RANK // 8)], axis=0)
            for k in range(width)
        ]
        out = dot3(low, split(jnp.concatenate(columns, axis=1)), NN)
        for k in range(width):
            one = out[:, 128 * k : 128 * k + 128]
            squared = squared + one * one
        rhi[:, cut], rlo[:, cut] = split(out)
        for k, (buf, hbm) in enumerate(((rhi, high_hbm), (rlo, low_hbm))):
            stores.append(pltpu.make_async_copy(buf.at[:, cut], hbm.at[:, cut], store_sem.at[2 * n + k]))
            stores[-1].start()
    nbuf[t] = dot_full(jnp.ones((8, 128), F32), squared, NT)

    if nt > 1:
        def send_norm(r, carry):
            remote(
                nbuf.at[t], nbuf.at[t], s_send.at[6], s_recv.at[6], (f, tmod(t + r))
            ).start()
            return carry

        lax.fori_loop(1, nt, send_norm, 0)

    ortho = ortho_f32[...]
    ortho_out[...] = ortho.astype(BF16)
    if nt > 1:
        wait(nbuf.at[pl.ds(0, nt - 1)], s_recv.at[6])
    norm = nbuf[0]
    for r in range(1, nt):
        norm = norm + nbuf[r]
    inverse = 1.0 / (jnp.sqrt(norm) + 1e-06)
    scaled_high[...], scaled_low[...] = split(ortho * (inverse[0:1, :] * -factor))
    for store in stores:
        store.wait()
    for buf, sem in ((vbuf, v_send), (wbuf, r_send), (wfin, w_send)):
        wait(buf.at[pl.ds(0, (nz * NX - 1) * m)], sem.at[0])
    if nt > 1:
        wait(rsbuf, s_send.at[0])
        wait(proj.at[pl.ds(0, (nt - 1) * share)], s_send.at[1])
        wait(gall.at[pl.ds(0, (nt - 1) * ng)], s_send.at[5])
        wait(nbuf.at[pl.ds(0, nt - 1)], s_send.at[6])
    wait(grs, s_send.at[2])
    wait(gx.at[pl.ds(0, NX - 1)], s_send.at[3])
    wait(gall.at[pl.ds(0, (nz - 1) * mg)], s_send.at[4])


def update(
    mom_hbm, grad_hbm, high_hbm, low_hbm, ortho, scaled_high, scaled_low, newm_hbm, delta_hbm,
    mom, grad, rhi, rlo, dout, load_sem, store_sem,
):
    cuts = cuts_of(mom.shape[1] // 256)
    nh = mom.shape[1] // 256
    pairs = ((high_hbm, rhi), (low_hbm, rlo), (mom_hbm, mom), (grad_hbm, grad))
    loads, stores = [], []
    for n, (h, start, width) in enumerate(cuts):
        cut = slice((h * nh + start) * 128, (h * nh + start + width) * 128)
        for k, (hbm, buf) in enumerate(pairs):
            loads.append(pltpu.make_async_copy(hbm.at[:, cut], buf.at[:, cut], load_sem.at[4 * n + k]))
            loads[-1].start()
    both = jnp.concatenate([scaled_high[...], scaled_low[...], ortho[...]], axis=0)
    rows = ortho.shape[0]
    for n, (h, start, width) in enumerate(cuts):
        cut = slice((h * nh + start) * 128, (h * nh + start + width) * 128)
        for load in loads[4 * n : 4 * n + 4]:
            load.wait()
        high = dot(both, rhi[:, cut], NN)
        delta = high[:rows] + (high[rows : 2 * rows] + dot(scaled_high[...], rlo[:, cut], NN))
        dout[:, cut] = delta.astype(BF16)
        mom[:, cut] = (mom[:, cut] + grad[:, cut].astype(F32)) - 0.05 * high[2 * rows :]
        for k, (buf, hbm) in enumerate(((mom, newm_hbm), (dout, delta_hbm))):
            stores.append(pltpu.make_async_copy(buf.at[:, cut], hbm.at[:, cut], store_sem.at[2 * n + k]))
            stores[-1].start()
    for store in stores:
        store.wait()


def per_device(nz, nt, factor, momentum, gradient, basis):
    rows, cols = momentum.shape
    nblk = cols // 128
    nh = nblk // 2
    m = GROUPS // (nz * NX)
    gshare = RANK // nt
    ng = 2 * gshare // 4
    mg = ng // nz
    na = min(NA, nh - 1)
    nb = nh - na
    tiles = basis.reshape(m, 4, nblk, 128).transpose(0, 2, 1, 3)
    vmem = pltpu.VMEM
    dma = pltpu.SemaphoreType.DMA
    any_spec = pl.BlockSpec(memory_space=pl.ANY)
    one = max(nt - 1, 1)
    vmem_spec = pl.BlockSpec(memory_space=pltpu.VMEM)
    ncut = len(cuts_of(nh))
    high, low, ortho, scaled_high, scaled_low = pl.pallas_call(
        functools.partial(kernel, nz, nt, factor),
        out_shape=(
            jax.ShapeDtypeStruct((RANK, cols), BF16),
            jax.ShapeDtypeStruct((RANK, cols), BF16),
            jax.ShapeDtypeStruct((rows, RANK), BF16),
            jax.ShapeDtypeStruct((rows, RANK), BF16),
            jax.ShapeDtypeStruct((rows, RANK), BF16),
        ),
        in_specs=[any_spec] * 3,
        out_specs=(any_spec, any_spec, vmem_spec, vmem_spec, vmem_spec),
        scratch_shapes=[
            vmem((rows, cols), F32),
            vmem((rows, cols), BF16),
            vmem((rows, cols), BF16),
            vmem((rows, cols), BF16),
            vmem((GROUPS, nblk, 4, 128), F32),
            vmem((rows, RANK), F32),
            vmem((rows, RANK), F32),
            vmem((one, rows // nt, RANK), F32),
            vmem((GROUPS, nh, 8, 128), F32),
            vmem((nz * m, nb, 8, 128), F32),
            vmem((nz * m, nb, 8, 128), F32),
            vmem((nz * m, nb, 8, 128), F32),
            vmem(((nz + 1) * m, nb, 8, 128), F32),
            vmem(((nz + 1) * m, nb, 8, 128), F32),
            vmem(((nz + 1) * NX * m, na, 8, 128), F32),
            vmem(((nz + 1) * NX * m, na, 8, 128), F32),
            vmem((NX * m, na, 8, 128), F32),
            vmem((GROUPS, nh, 8, 128), F32),
            vmem((RANK, RANK), F32),
            vmem((ng, 4, 128), F32),
            vmem((nz - 1, mg, 4, 128), F32),
            vmem((mg, 4, 128), F32),
            vmem((NX, mg, 4, 128), F32),
            vmem((2 * GROUPS, 4, 128), F32),
            vmem((RANK, 2 * RANK), F32),
            vmem((RANK, cols), BF16),
            vmem((RANK, cols), BF16),
            vmem((nt, 8, RANK), F32),
            vmem((rows, RANK), F32),
            vmem((RANK, RANK), BF16),
            vmem((RANK, RANK), BF16),
            dma((3,)),
            dma((2 * ncut,)),
            dma((1,)), dma((nz,)), dma((nz,)), dma((nz,)), dma((nz,)), dma((nz + 1,)),
            dma((1,)), dma((nz,)), dma((nz,)), dma((nz,)), dma((nz,)), dma((nz + 1,)),
            dma((1,)), dma((nz + 1,)), dma((nz + 1,)), dma((nz + 2,)), dma((nz + 1,)),
            dma((nz,)), dma((nz,)), dma((nz,)),
            dma((7,)),
            dma((7,)),
        ],
        compiler_params=pltpu.CompilerParams(
            collective_id=0, has_side_effects=True, vmem_limit_bytes=56 * 2**20
        ),
        name="dion_step",
    )(momentum, gradient, tiles)
    return pl.pallas_call(
        update,
        out_shape=(
            jax.ShapeDtypeStruct((rows, cols), F32),
            jax.ShapeDtypeStruct((rows, cols), BF16),
        ),
        in_specs=[any_spec] * 4 + [vmem_spec] * 3,
        out_specs=(any_spec, any_spec),
        scratch_shapes=[
            vmem((rows, cols), F32),
            vmem((rows, cols), BF16),
            vmem((RANK, cols), BF16),
            vmem((RANK, cols), BF16),
            vmem((rows, cols), BF16),
            dma((4 * ncut,)),
            dma((2 * ncut,)),
        ],
        compiler_params=pltpu.CompilerParams(vmem_limit_bytes=56 * 2**20),
        name="dion_update",
    )(momentum, gradient, high, low, ortho, scaled_high, scaled_low)


def solution(mesh):
    nz, nt = mesh.shape["fsdp"] // NX, mesh.shape["tensor"]
    factor = (ROWS * COLS / RANK) ** 0.5
    spec = P("fsdp", "tensor")
    return jax.shard_map(
        functools.partial(per_device, nz, nt, factor),
        mesh=mesh, in_specs=(spec,) * 3, out_specs=(spec,) * 2, check_vma=False,
    )
```

```python
import functools

import jax
import jax.numpy as jnp
from jax import lax
from jax.experimental import pallas as pl
from jax.experimental.pallas import tpu as pltpu
from jax.sharding import PartitionSpec as P

ROWS = 8192
COLS = 26624
RANK = 256
NX = 4
GROUPS = RANK // 4
PANEL = 32
MINI = 16
NA = 2
LAG = 2
LAG_A = 2
UNROLL = 13
LAG_S = 1
LAG_B = 1
LAG_C = 3
GRAM_AT = (2, 4, 6, 9)
F32 = jnp.float32
BF16 = jnp.bfloat16
HIGHEST = lax.Precision.HIGHEST
NT = (((1,), (1,)), ((), ()))
TN = (((0,), (0,)), ((), ()))
NN = (((1,), (0,)), ((), ()))


def split3(value):
    high = value.astype(BF16)
    rest = value - high.astype(F32)
    mid = rest.astype(BF16)
    return high, mid, (rest - mid.astype(F32)).astype(BF16)


def split(value):
    high = value.astype(BF16)
    return high, (value - high.astype(F32)).astype(BF16)


def dot(a, b, dims):
    return lax.dot_general(a, b, dims, preferred_element_type=F32)


def dot3(a, b, dims):
    (ah, al), (bh, bl) = a, b
    return dot(ah, bh, dims) + (dot(ah, bl, dims) + dot(al, bh, dims))


def dot_full(a, b, dims):
    return lax.dot_general(a, b, dims, precision=HIGHEST, preferred_element_type=F32)


def cuts_of(nh):
    cuts = []
    for h in range(2):
        start = 0
        while start < nh:
            width = min(4, nh - start) if nh - start != 5 else 5
            cuts.append((h, start, width))
            start += width
    return cuts


def kernel(
    nz, nt, factor,
    mom_hbm, grad_hbm, basis_hbm, high_hbm, low_hbm, ortho_out, scaled_high, scaled_low,
    mom, grad, bhi, blo, vbuf, part, proj, rsbuf,
    wbuf, ropp, rleft, rright, rodd, reven, aodd, aeven, across, wfin,
    gram, gslice, grs, gsum, gx, gall, elim,
    rhi, rlo, nbuf, ortho_f32, lhi, llo,
    load_sem, store_sem, v_send, v_z, v_l, v_r, v_o, v_a,
    w_send, w_z, w_l, w_r, w_o, w_a, r_send, r_odd, r_even, a_odd, a_even, r_l, r_r, r_o,
    s_send, s_recv,
):
    rows, cols = mom.shape
    nblk = cols // 128
    nh = nblk // 2
    half = nz // 2
    na = across.shape[1]
    nb = nh - na
    m = GROUPS // (nz * NX)
    f = lax.axis_index("fsdp")
    t = lax.axis_index("tensor")
    z, x = lax.div(f, NX), lax.rem(f, NX)
    left, right, opp = lax.rem(x + NX - 1, NX), lax.rem(x + 1, NX), lax.rem(x + 2, NX)

    def zmod(value):
        return lax.rem(value + nz, nz)

    def tmod(value):
        return lax.rem(value + nt, nt)

    def dev(zz, xx):
        return (zz * NX + xx, t)

    def far_t(r):
        return lax.rem(r + max(nt // 4 - 1, 0), max(nt - 1, 1)) + 1

    def far_z(r):
        return lax.rem(r + half - 2, nz - 1) + 1

    to_up, to_down = dev(zmod(z + 1), x), dev(zmod(z - 1), x)
    to_up2, to_down2 = dev(zmod(z + 2), x), dev(zmod(z - 2 + nz), x)
    to_left, to_right, to_opp = dev(z, left), dev(z, right), dev(z, opp)

    def remote(src, dst, send, recv, device):
        return pltpu.make_async_remote_copy(
            src_ref=src, dst_ref=dst, send_sem=send, recv_sem=recv,
            device_id=device, device_id_type=pl.DeviceIdType.MESH,
        )

    def wait(ref, sem):
        pltpu.make_async_copy(ref, ref, sem).wait()

    load_basis = pltpu.make_async_copy(basis_hbm, vbuf.at[pl.ds(f * m, m)], load_sem.at[0])
    load_mom = pltpu.make_async_copy(mom_hbm, mom, load_sem.at[1])
    load_grad = pltpu.make_async_copy(grad_hbm, grad, load_sem.at[2])
    load_basis.start()
    load_mom.start()
    load_grad.start()

    barrier = pltpu.get_barrier_semaphore()

    def greet(device):
        pl.semaphore_signal(barrier, inc=1, device_id=device, device_id_type=pl.DeviceIdType.MESH)

    def greet_t(r, carry):
        greet((f, tmod(t + r)))
        return carry

    lax.fori_loop(1, nt, greet_t, 0)
    near = [to_left, to_right, to_opp]
    near += [dev(zmod(z + r), x) for r in sorted({1 % nz, nz - 1, 2 % nz, nz - 2} - {0})]
    for device in near:
        greet(device)
    pl.semaphore_wait(barrier, (nt - 1) + len(near))

    def gather(buf, cut, send, sz, sl, sr, so, sa, early, hook, tail):
        whole = buf.shape[1]

        def at(zz, xx):
            return buf.at[pl.ds((zz * NX + xx) * m, m), pl.ds(0, cut)]

        def late(zz, xx):
            return buf.at[pl.ds((zz * NX + xx) * m, m), pl.ds(cut, whole - cut)]

        def bundle(zz):
            return buf.at[pl.ds(zz * NX * m, NX * m), pl.ds(cut, whole - cut)]

        def onward(j, ref, sem):
            @pl.when(j + 2 <= half)
            def _():
                remote(ref, ref, send, sem, to_up2).start()

            @pl.when(j + 1 <= half)
            def _():
                remote(ref, ref, send, sem, to_up).start()

        def back(j, ref, sem):
            @pl.when(j + 2 < half)
            def _():
                remote(ref, ref, send, sem, to_down2).start()

            @pl.when(j + 1 < half)
            def _():
                remote(ref, ref, send, sem, to_down).start()

        def push(zz, xx, sem, device):
            remote(at(zz, xx), at(zz, xx), send, sem.at[zz], device).start()

        def spread(zz):
            push(zz, x, sl, to_right)
            push(zz, x, sr, to_left)

        def pass_right(zz):
            wait(at(zz, left), sl.at[zz])
            push(zz, left, so, to_right)

        def pass_left(zz):
            wait(at(zz, right), sr.at[zz])
            push(zz, right, so, to_left)

        def late_ones(j):
            below, above = zmod(z - j), zmod(z + j)
            even = lax.rem(j, 2) == 0

            @pl.when((j > 0) & (j <= half))
            def _():
                wait(bundle(below), sa.at[below])
                pl.when(even)(lambda: onward(j, bundle(below), sa.at[below]))

            @pl.when((j > 0) & (j < half))
            def _():
                wait(bundle(above), sa.at[above])
                pl.when(even)(lambda: back(j, bundle(above), sa.at[above]))

        def passing(j):
            @pl.when(j == 0)
            def _():
                pass_left(z)

            @pl.when((j > 0) & (j < half))
            def _():
                pass_right(zmod(z - j))
                pass_left(zmod(z + j))

        for device in (to_right, to_left, to_opp):
            remote(late(z, x), late(z, x), send, sa.at[nz], device).start()
        onward(0, at(z, x), sz.at[z])
        back(0, at(z, x), sz.at[z])
        spread(z)
        early()
        wait(buf.at[pl.ds(0, (NX - 1) * m), pl.ds(cut, whole - cut)], sa.at[nz])
        onward(0, bundle(z), sa.at[z])
        back(0, bundle(z), sa.at[z])

        def step(j, carry):
            below, above = zmod(z - j), zmod(z + j)
            even = lax.rem(j, 2) == 0
            wait(at(below, x), sz.at[below])

            @pl.when(even)
            def _():
                onward(j, at(below, x), sz.at[below])

            @pl.when(j < half)
            def _():
                wait(at(above, x), sz.at[above])

                @pl.when(even)
                def _():
                    back(j, at(above, x), sz.at[above])

            spread(below)

            @pl.when(j < half)
            def _():
                spread(above)

            pl.when(j == half)(lambda: push(below, x, so, to_opp))
            late_ones(j - LAG_A)
            passing(j - LAG)
            hook(j)
            return carry

        lax.fori_loop(1, half + 1, step, 0)
        rest = max(LAG, LAG_A)

        def drain(j, carry):
            late_ones(j - LAG_A)
            passing(j - LAG)
            return carry

        lax.fori_loop(half + 1, half + 1 + rest, drain, 0)

        def finish(j, carry):
            below, above = zmod(z - j), zmod(z + j)
            wait(at(below, opp), so.at[below])
            pl.when(j > 0)(lambda: wait(at(below, right), sr.at[below]))
            pl.when((j == 0) | (j == half))(lambda: wait(at(below, left), sl.at[below]))

            @pl.when((j > 0) & (j < half))
            def _():
                wait(at(above, left), sl.at[above])
                wait(at(above, opp), so.at[above])

            return carry

        tail()
        lax.fori_loop(0, half + 1, finish, 0)

    load_basis.wait()

    def make_blend():
        load_mom.wait()
        load_grad.wait()

        def body(c, carry):
            cut = pl.ds(pl.multiple_of(c * 256, 256), 256)
            blend = mom[:, cut] + grad[:, cut].astype(F32)
            mom[:, cut] = blend
            bhi[:, cut], blo[:, cut] = split(blend)
            return carry

        lax.fori_loop(0, nblk // 2, body, 0)

    gather(vbuf, 2 * nb, v_send.at[0], v_z, v_l, v_r, v_o, v_a, make_blend, lambda j: None, lambda: None)

    def project(c, acc):
        cut = pl.ds(pl.multiple_of(c * 256, 256), 256)
        pair = [vbuf[:, 2 * c + k].reshape(RANK, 128) for k in range(2)]
        return acc + dot3((bhi[:, cut], blo[:, cut]), split(jnp.concatenate(pair, axis=1)), NT)

    part[...] = lax.fori_loop(0, nblk // 2, project, jnp.zeros((rows, RANK), F32), unroll=UNROLL)

    share = rows // nt
    if nt > 1:
        own = pl.ds(t * share, share)

        def send_part(r, carry):
            r = far_t(r)
            peer = tmod(t + r)
            remote(
                part.at[pl.ds(peer * share, share)], rsbuf.at[r - 1],
                s_send.at[0], s_recv.at[0], (f, peer),
            ).start()
            return carry

        lax.fori_loop(1, nt, send_part, 0)
        wait(rsbuf, s_recv.at[0])
        total = part[own]
        for r in range(nt - 1):
            total = total + rsbuf[r]
        proj[own] = total

        def send_sum(r, carry):
            remote(
                proj.at[own], proj.at[own], s_send.at[1], s_recv.at[1], (f, tmod(t + far_t(r)))
            ).start()
            return carry

        lax.fori_loop(1, nt, send_sum, 0)
        wait(proj.at[pl.ds(0, (nt - 1) * share)], s_recv.at[1])
    else:
        proj[...] = part[...]

    full = proj[...]
    gshare = RANK // nt
    ng = 2 * gshare // 4
    mg = ng // nz

    def make_gram():
        square = proj[...]
        gram[...] = dot_full(square, square, TN)
        mine = gram[pl.ds(t * gshare, gshare), :]
        for r in range(gshare // 4):
            for c in range(2):
                gslice[2 * r + c] = mine[4 * r : 4 * r + 4, 128 * c : 128 * c + 128]

    def gram_send():
        make_gram()

        def body(r, carry):
            r = far_z(r)
            peer = zmod(z + r)
            remote(
                gslice.at[pl.ds(peer * mg, mg)], grs.at[r - 1],
                s_send.at[2], s_recv.at[2], dev(peer, x),
            ).start()
            return carry

        lax.fori_loop(1, nz, body, 0)

    def gram_over_z():
        wait(grs, s_recv.at[2])
        gsum[...] = gslice[pl.ds(z * mg, mg)] + jnp.sum(grs[...], axis=0)
        gx[x] = gsum[...]
        for k, device in enumerate((to_left, to_right, to_opp)):
            remote(gsum, gx.at[x], s_send.at[3], s_recv.at[3], device).start()

    def gram_over_x():
        wait(gx.at[pl.ds(0, NX - 1)], s_recv.at[3])
        here = pl.ds(t * ng + z * mg, mg)
        gall[here] = jnp.sum(gx[...], axis=0)

        def body(r, carry):
            remote(
                gall.at[here], gall.at[here], s_send.at[4], s_recv.at[4], dev(zmod(z + far_z(r)), x)
            ).start()
            return carry

        lax.fori_loop(1, nz, body, 0)

    def gram_over_t():
        wait(gall.at[pl.ds(0, (nz - 1) * mg)], s_recv.at[4])
        if nt > 1:
            here = pl.ds(t * ng, ng)

            def body(r, carry):
                remote(
                    gall.at[here], gall.at[here], s_send.at[5], s_recv.at[5], (f, tmod(t + far_t(r)))
                ).start()
                return carry

            lax.fori_loop(1, nt, body, 0)

    def gram_done():
        if nt > 1:
            wait(gall.at[pl.ds(0, (nt - 1) * ng)], s_recv.at[5])
        for r in range(RANK // 8):
            for c in range(2):
                pair = [gall[4 * r + c], gall[4 * r + 2 + c]]
                elim[8 * r : 8 * r + 8, 128 * c : 128 * c + 128] = jnp.concatenate(pair, axis=0)
        down = lax.broadcasted_iota(jnp.int32, (RANK, RANK), 0)
        across = lax.broadcasted_iota(jnp.int32, (RANK, RANK), 1)
        elim[:, RANK:] = jnp.where(down == across, 1.0, 0.0).astype(F32)

    turned = split(full.T)
    for h, start, width in cuts_of(nh):
        cut = slice((h * nh + start) * 128, (h * nh + start + width) * 128)
        out = dot3(turned, (bhi[:, cut], blo[:, cut]), NN)
        for k in range(width):
            for r in range(RANK // 8):
                wbuf[2 * r + h, start + k] = out[8 * r : 8 * r + 8, 128 * k : 128 * k + 128]

    def piece(buf, index):
        return buf.at[pl.ds(index * m, m)]

    def wat(q, xx):
        return wbuf.at[pl.ds((q * NX + xx) * m, m), pl.ds(0, nb)]

    def wlate(q, xx):
        return wbuf.at[pl.ds((q * NX + xx) * m, m), pl.ds(nb, na)]

    def wbundle(q):
        return wbuf.at[pl.ds(q * NX * m, NX * m), pl.ds(nb, na)]

    def slots(buf, index):
        return buf.at[pl.ds(index * NX * m, NX * m)]

    def add_into(ref, other):
        ref[...] = ref[...] + other[...]

    def stage_a(q, s):
        remote(wat(q, opp), piece(ropp, q), r_send.at[0], r_o.at[q], (to_right, to_left, to_opp)[s]).start()

    def stage_b(q, s):
        if s < 2:
            wait(piece(ropp, q), r_o.at[q])
            add_into(wat(q, (right, left)[s]), piece(ropp, q))
        remote(wat(q, right), piece(rleft, q), r_send.at[0], r_l.at[q], to_right).start()
        remote(wat(q, left), piece(rright, q), r_send.at[0], r_r.at[q], to_left).start()

    def stage_c(q):
        wait(piece(rleft, q), r_l.at[q])
        wait(piece(rright, q), r_r.at[q])
        here = wat(q, x)
        here[...] = here[...] + (piece(rleft, q)[...] + piece(rright, q)[...])

    def z_sum(j, top, q, ref, place, odd, even, s_odd, s_even, to_one, to_two, up):
        def slot(last):
            return jnp.where(last, nz, q) if up else q

        is_odd = lax.rem(j, 2) == 1

        @pl.when(is_odd & (j <= top))
        def _():
            at = slot(j == 1)
            remote(ref, place(odd, at), r_send.at[0], s_odd.at[at], to_one).start()

        @pl.when(jnp.logical_not(is_odd) & (j >= 2) & (j <= top))
        def _():
            @pl.when(j + 1 <= top)
            def _():
                wait(place(odd, q), s_odd.at[q])
                add_into(ref, place(odd, q))

            @pl.when(j + 2 <= top)
            def _():
                wait(place(even, q), s_even.at[q])
                add_into(ref, place(even, q))

            at = slot(j == 2)
            remote(ref, place(even, at), r_send.at[0], s_even.at[at], to_two).start()

    def z_last(ref, place, odd, even, s_odd, s_even):
        for buf, sem, index, there in (
            (odd, s_odd, z, half >= 1), (even, s_even, z, half >= 2),
            (odd, s_odd, nz, half >= 2), (even, s_even, nz, half >= 3),
        ):
            if there:
                wait(place(buf, index), sem.at[index])
                add_into(ref, place(buf, index))

    def early_sum(j):
        args = (slots, aodd, aeven, a_odd, a_even)
        q = zmod(z - j)
        z_sum(j, half, q, wbundle(q), *args, to_down, to_down2, False)
        q = zmod(z + j)
        z_sum(j, half - 1, q, wbundle(q), *args, to_up, to_up2, True)

        @pl.when(j == 0)
        def _():
            z_last(wbundle(z), *args)
            for xx, device in ((left, to_left), (right, to_right), (opp, to_opp)):
                remote(wlate(z, xx), piece(across, x), r_send.at[0], a_odd.at[nz + 1], device).start()
            piece(across, x)[...] = wlate(z, x)[...]

    def late_sum(j):
        args = (piece, rodd, reven, r_odd, r_even)
        q = zmod(z - j)
        stage_c(q)

        @pl.when(j == half)
        def _():
            wait(piece(ropp, q), r_o.at[q])
            add_into(wat(q, x), piece(ropp, q))

        z_sum(j, half, q, wat(q, x), *args, to_down, to_down2, False)

        @pl.when((j >= 1) & (j < half))
        def _():
            q = zmod(z + j)
            stage_c(q)
            z_sum(j, half - 1, q, wat(q, x), *args, to_up, to_up2, True)

        @pl.when(j == 0)
        def _():
            z_last(wat(z, x), *args)

    lane = lax.broadcasted_iota(jnp.int32, (PANEL, 128), 1)
    down = lax.broadcasted_iota(jnp.int32, (PANEL, 128), 0)
    wide = lax.broadcasted_iota(jnp.int32, (PANEL, RANK), 1)
    npanel = RANK // PANEL

    def panel(b):
        here = pl.ds(pl.multiple_of(b * PANEL, PANEL), PANEL)
        block = elim[here, :]
        turned = pltpu.roll(block[:, :RANK], lax.rem(RANK - b * PANEL, RANK), 1)[:, :128]
        state = jnp.where(lane < PANEL, turned, jnp.where(lane == down + PANEL, 1.0, 0.0))
        for first in range(0, PANEL, MINI):
            spread = [
                jnp.broadcast_to(state[:, k : k + 1], (PANEL, 128)) for k in range(first, first + MINI)
            ]
            for k in range(min(MINI, PANEL - 1 - first)):
                j = first + k
                scale = jnp.where(down > j, spread[k], 0.0) * (1.0 / spread[k][j : j + 1, :])
                state = state - scale * state[j : j + 1, :]
                for n in range(k + 1, MINI):
                    spread[n] = spread[n] - scale * spread[n][j : j + 1, :]
        diag = jnp.sum(jnp.where(lane == down, state, 0.0), axis=1, keepdims=True)
        lower = state[:, PANEL : 2 * PANEL] / jnp.sqrt(diag)
        done = dot_full(lower, block, NN)
        rest = jnp.where(wide >= (b + 1) * PANEL, done[:, :RANK], 0.0)
        (rh, rm, rl), (dh, dm, dl) = split3(rest), split3(done)
        elim[...] = elim[...] - dot(
            jnp.concatenate([rh, rh, rh, rm, rm, rl], axis=0),
            jnp.concatenate([dh, dm, dl, dh, dm, dh], axis=0),
            TN,
        )
        elim[here, :] = done

    def reduce_step(i, carry):
        @pl.when(i == 0)
        def _():
            q = zmod(z - half)
            stage_a(q, 2)
            stage_b(q, 2)

        @pl.when((i >= 1) & (i < half))
        def _():
            stage_a(zmod(z - half + i), 0)

        @pl.when((i >= 1) & (i <= half))
        def _():
            stage_a(zmod(z + half - i), 1)

        @pl.when(i >= LAG_C)
        def _():
            late_sum(half + LAG_C - i)

        @pl.when((i >= LAG_S) & (i <= half + LAG_S))
        def _():
            early_sum(half + LAG_S - i)

        b = i - LAG_B

        @pl.when((b >= 1) & (b < half))
        def _():
            stage_b(zmod(z - half + b), 0)

        @pl.when((b >= 1) & (b <= half))
        def _():
            stage_b(zmod(z + half - b), 1)

        pl.when(i == 0)(gram_send)
        last = half + LAG_C
        for place, work in zip(GRAM_AT, (gram_over_z, gram_over_x, gram_over_t, gram_done)):
            pl.when(i == min(place, last))(work)

        @pl.when(i > max(GRAM_AT))
        def _():
            panel(i - max(GRAM_AT) - 1)

        return carry

    lax.fori_loop(0, half + 1 + LAG_C, reduce_step, 0)
    wait(across.at[pl.ds(0, (NX - 1) * m)], a_odd.at[nz + 1])
    wfin[pl.ds(f * m, m), 0:nb] = wat(z, x)[...]
    wfin[pl.ds(f * m, m), nb:] = jnp.sum(across[...].reshape(NX, m, na, 8, 128), axis=0)

    def make_ortho():
        inv_lower = elim[:, RANK:]
        ortho_f32[...] = dot_full(proj[...], inv_lower, NT)
        lhi[...], llo[...] = split(inv_lower)

    begun = max(0, half + LAG_C - max(GRAM_AT))

    def panels(j):
        per = -(-(npanel - begun) // max(half // 2, 1))

        @pl.when(lax.rem(j, 2) == (0 if half > 1 else 1))
        def _():
            for k in range(per):
                b = begun + (lax.div(j, 2) - (1 if half > 1 else 0)) * per + k
                pl.when(b < npanel)(functools.partial(panel, b))

    gather(wfin, nb, w_send.at[0], w_z, w_l, w_r, w_o, w_a, lambda: None, panels, make_ortho)

    low = lhi[...], llo[...]
    squared = jnp.zeros((RANK, 128), F32)
    stores = []
    for n, (h, start, width) in enumerate(cuts_of(nh)):
        cut = slice((h * nh + start) * 128, (h * nh + start + width) * 128)
        columns = [
            jnp.concatenate([wfin[2 * r + h, start + k] for r in range(RANK // 8)], axis=0)
            for k in range(width)
        ]
        out = dot3(low, split(jnp.concatenate(columns, axis=1)), NN)
        for k in range(width):
            one = out[:, 128 * k : 128 * k + 128]
            squared = squared + one * one
        rhi[:, cut], rlo[:, cut] = split(out)
        for k, (buf, hbm) in enumerate(((rhi, high_hbm), (rlo, low_hbm))):
            stores.append(pltpu.make_async_copy(buf.at[:, cut], hbm.at[:, cut], store_sem.at[2 * n + k]))
            stores[-1].start()
    nbuf[t] = dot_full(jnp.ones((8, 128), F32), squared, NT)

    if nt > 1:
        def send_norm(r, carry):
            remote(
                nbuf.at[t], nbuf.at[t], s_send.at[6], s_recv.at[6], (f, tmod(t + far_t(r)))
            ).start()
            return carry

        lax.fori_loop(1, nt, send_norm, 0)

    ortho = ortho_f32[...]
    ortho_out[...] = ortho.astype(BF16)
    if nt > 1:
        wait(nbuf.at[pl.ds(0, nt - 1)], s_recv.at[6])
    norm = nbuf[0]
    for r in range(1, nt):
        norm = norm + nbuf[r]
    inverse = 1.0 / (jnp.sqrt(norm) + 1e-06)
    scaled_high[...], scaled_low[...] = split(ortho * (inverse[0:1, :] * -factor))
    for store in stores:
        store.wait()
    for buf, sem in ((vbuf, v_send), (wbuf, r_send), (wfin, w_send)):
        wait(buf.at[pl.ds(0, (nz * NX - 1) * m)], sem.at[0])
    if nt > 1:
        wait(rsbuf, s_send.at[0])
        wait(proj.at[pl.ds(0, (nt - 1) * share)], s_send.at[1])
        wait(gall.at[pl.ds(0, (nt - 1) * ng)], s_send.at[5])
        wait(nbuf.at[pl.ds(0, nt - 1)], s_send.at[6])
    wait(grs, s_send.at[2])
    wait(gx.at[pl.ds(0, NX - 1)], s_send.at[3])
    wait(gall.at[pl.ds(0, (nz - 1) * mg)], s_send.at[4])


def update(
    mom_hbm, grad_hbm, high_hbm, low_hbm, ortho, scaled_high, scaled_low, newm_hbm, delta_hbm,
    mom, grad, rhi, rlo, dout, load_sem, store_sem,
):
    cuts = cuts_of(mom.shape[1] // 256)
    nh = mom.shape[1] // 256
    pairs = ((high_hbm, rhi), (low_hbm, rlo), (mom_hbm, mom), (grad_hbm, grad))
    loads, stores = [], []
    for n, (h, start, width) in enumerate(cuts):
        cut = slice((h * nh + start) * 128, (h * nh + start + width) * 128)
        for k, (hbm, buf) in enumerate(pairs):
            loads.append(pltpu.make_async_copy(hbm.at[:, cut], buf.at[:, cut], load_sem.at[4 * n + k]))
            loads[-1].start()
    both = jnp.concatenate([scaled_high[...], scaled_low[...], ortho[...]], axis=0)
    rows = ortho.shape[0]
    for n, (h, start, width) in enumerate(cuts):
        cut = slice((h * nh + start) * 128, (h * nh + start + width) * 128)
        for load in loads[4 * n : 4 * n + 4]:
            load.wait()
        high = dot(both, rhi[:, cut], NN)
        delta = high[:rows] + (high[rows : 2 * rows] + dot(scaled_high[...], rlo[:, cut], NN))
        dout[:, cut] = delta.astype(BF16)
        mom[:, cut] = (mom[:, cut] + grad[:, cut].astype(F32)) - 0.05 * high[2 * rows :]
        for k, (buf, hbm) in enumerate(((mom, newm_hbm), (dout, delta_hbm))):
            stores.append(pltpu.make_async_copy(buf.at[:, cut], hbm.at[:, cut], store_sem.at[2 * n + k]))
            stores[-1].start()
    for store in stores:
        store.wait()


def per_device(nz, nt, factor, momentum, gradient, basis):
    rows, cols = momentum.shape
    nblk = cols // 128
    nh = nblk // 2
    m = GROUPS // (nz * NX)
    gshare = RANK // nt
    ng = 2 * gshare // 4
    mg = ng // nz
    na = min(NA, nh - 1)
    nb = nh - na
    tiles = basis.reshape(m, 4, nblk, 128).transpose(0, 2, 1, 3)
    vmem = pltpu.VMEM
    dma = pltpu.SemaphoreType.DMA
    any_spec = pl.BlockSpec(memory_space=pl.ANY)
    one = max(nt - 1, 1)
    vmem_spec = pl.BlockSpec(memory_space=pltpu.VMEM)
    ncut = len(cuts_of(nh))
    high, low, ortho, scaled_high, scaled_low = pl.pallas_call(
        functools.partial(kernel, nz, nt, factor),
        out_shape=(
            jax.ShapeDtypeStruct((RANK, cols), BF16),
            jax.ShapeDtypeStruct((RANK, cols), BF16),
            jax.ShapeDtypeStruct((rows, RANK), BF16),
            jax.ShapeDtypeStruct((rows, RANK), BF16),
            jax.ShapeDtypeStruct((rows, RANK), BF16),
        ),
        in_specs=[any_spec] * 3,
        out_specs=(any_spec, any_spec, vmem_spec, vmem_spec, vmem_spec),
        scratch_shapes=[
            vmem((rows, cols), F32),
            vmem((rows, cols), BF16),
            vmem((rows, cols), BF16),
            vmem((rows, cols), BF16),
            vmem((GROUPS, nblk, 4, 128), F32),
            vmem((rows, RANK), F32),
            vmem((rows, RANK), F32),
            vmem((one, rows // nt, RANK), F32),
            vmem((GROUPS, nh, 8, 128), F32),
            vmem((nz * m, nb, 8, 128), F32),
            vmem((nz * m, nb, 8, 128), F32),
            vmem((nz * m, nb, 8, 128), F32),
            vmem(((nz + 1) * m, nb, 8, 128), F32),
            vmem(((nz + 1) * m, nb, 8, 128), F32),
            vmem(((nz + 1) * NX * m, na, 8, 128), F32),
            vmem(((nz + 1) * NX * m, na, 8, 128), F32),
            vmem((NX * m, na, 8, 128), F32),
            vmem((GROUPS, nh, 8, 128), F32),
            vmem((RANK, RANK), F32),
            vmem((ng, 4, 128), F32),
            vmem((nz - 1, mg, 4, 128), F32),
            vmem((mg, 4, 128), F32),
            vmem((NX, mg, 4, 128), F32),
            vmem((2 * GROUPS, 4, 128), F32),
            vmem((RANK, 2 * RANK), F32),
            vmem((RANK, cols), BF16),
            vmem((RANK, cols), BF16),
            vmem((nt, 8, RANK), F32),
            vmem((rows, RANK), F32),
            vmem((RANK, RANK), BF16),
            vmem((RANK, RANK), BF16),
            dma((3,)),
            dma((2 * ncut,)),
            dma((1,)), dma((nz,)), dma((nz,)), dma((nz,)), dma((nz,)), dma((nz + 1,)),
            dma((1,)), dma((nz,)), dma((nz,)), dma((nz,)), dma((nz,)), dma((nz + 1,)),
            dma((1,)), dma((nz + 1,)), dma((nz + 1,)), dma((nz + 2,)), dma((nz + 1,)),
            dma((nz,)), dma((nz,)), dma((nz,)),
            dma((7,)),
            dma((7,)),
        ],
        compiler_params=pltpu.CompilerParams(
            collective_id=0, has_side_effects=True, vmem_limit_bytes=56 * 2**20
        ),
        name="dion_step",
    )(momentum, gradient, tiles)
    return pl.pallas_call(
        update,
        out_shape=(
            jax.ShapeDtypeStruct((rows, cols), F32),
            jax.ShapeDtypeStruct((rows, cols), BF16),
        ),
        in_specs=[any_spec] * 4 + [vmem_spec] * 3,
        out_specs=(any_spec, any_spec),
        scratch_shapes=[
            vmem((rows, cols), F32),
            vmem((rows, cols), BF16),
            vmem((RANK, cols), BF16),
            vmem((RANK, cols), BF16),
            vmem((rows, cols), BF16),
            dma((4 * ncut,)),
            dma((2 * ncut,)),
        ],
        compiler_params=pltpu.CompilerParams(vmem_limit_bytes=56 * 2**20),
        name="dion_update",
    )(momentum, gradient, high, low, ortho, scaled_high, scaled_low)


def solution(mesh):
    nz, nt = mesh.shape["fsdp"] // NX, mesh.shape["tensor"]
    factor = (ROWS * COLS / RANK) ** 0.5
    spec = P("fsdp", "tensor")
    return jax.shard_map(
        functools.partial(per_device, nz, nt, factor),
        mesh=mesh, in_specs=(spec,) * 3, out_specs=(spec,) * 2, check_vma=False,
    )
```
